32 devices in a mesh: sec: 2 (over y), lat: 4 (over z), col: 4 (over x, core).
Axes of the slice: x: 2, y: 2, z: 4, core: 2. Of those that a mesh axis runs over, the one named last changes fastest.
Arguments:
- sources: bfloat16 [4, 16, 2, 128, 128], P('sec', ('lat', 'col')), may hold values from -6 to 6
- inverse_tiles: bfloat16 [4, 16, 8, 2, 128, 128], P('sec', 'lat', 'col'), may hold values from -0.15625 to 0.15625
- pattern: int32 [4, 16, 8], P('sec', 'lat', 'col'), may hold values 0 or 1
- phase_index: int32 [1], replicated, may hold values from 1 to 15
Outputs:
- solution: float32 [4, 16, 2, 128, 128], P('sec', ('lat', 'col'))
The draws below stay inside these ranges and needn't reach their ends.
All inputs are finite; a program needn't handle non-finite values. No bound on the sum of `pattern` on one device may be relied on, other than what follows from the above.
Results may differ from the reference program's by a relative error of at most 0.015.
Values may be sent and summed in bfloat16 or wider, within the bound.
No kernel may reach another device: no remote copies, remote signals or barrier semaphores. Data moves between devices by JAX's collectives and lax.ppermute only.
A program may use at most 64 MiB of HBM per device.

```python
import jax
import jax.numpy as jnp
from jax import lax

BLK = 128
OFF = 8
PHASES = 16
NRHS = 128
SLABS = 4
ROWBLK = 16


def with_ends(array, rng, smallest, high):
    longest = array.shape.index(max(array.shape))
    spots = []
    for shift in (0, 1):
        where = [jax.random.randint(jax.random.fold_in(rng, axis), (), 0, length) for axis, length in enumerate(array.shape)]
        where[longest] = (where[longest] + shift) % array.shape[longest]
        spots.append(tuple(where))
    return array.at[spots[0]].set(smallest).at[spots[1]].set(high)


def block_levels(key, extent, cuts, least, top_value):
    def one(axis_at, blocks):
        draws = jax.random.uniform(jax.random.fold_in(jax.random.fold_in(key, 6), axis_at), (blocks,), jnp.float32, least / len(cuts), top_value / len(cuts))
        return jnp.repeat(jnp.exp(draws), extent[axis_at] // blocks).reshape((-1,) + (1,) * (len(extent) - axis_at - 1))

    loudness = one(*cuts[0])
    for cut in cuts[1:]:
        loudness = loudness * one(*cut)
    return loudness


def bell_draw(own_key, dims, scale, bound, cuts=(), kind=jnp.bfloat16):
    values = jax.random.normal(own_key, dims, jnp.float32) * scale
    if len(cuts) > 0:
        values = block_levels(own_key, dims, cuts, -0.22, 0.18) * values
    return jnp.clip(values, min=-bound, max=bound).astype(kind)


def setup_inputs(seed: int = 0) -> dict:
    splits = jax.random.split(jax.random.key(seed), 5)
    sources = bell_draw(splits[0], (SLABS, ROWBLK, 2, BLK, NRHS), 1.0, 6.0, ((0, 2), (1, 16)))
    inverse_tiles = bell_draw(splits[1], (SLABS, ROWBLK, OFF, 2, BLK, BLK), (3 * BLK * OFF // 2) ** -0.5, 0.15625, ((0, 2), (1, 4), (2, 4)))
    pattern = with_ends((jax.random.randint(splits[2], (SLABS, ROWBLK, OFF), 0, 4) < 3).astype(jnp.int32), jax.random.fold_in(splits[2], 1), 0, 1)
    phase_index = jax.random.randint(splits[3], (1,), 1, PHASES).astype(jnp.int32)
    return {"sources": sources, "inverse_tiles": inverse_tiles, "pattern": pattern, "phase_index": phase_index}


coupling = 0.8


def rotated(part, cos_value, sin_value):
    wide = part.astype(jnp.float32)
    real_part = wide[:, 0] * cos_value - wide[:, 1] * sin_value
    imag_part = wide[:, 0] * sin_value + wide[:, 1] * cos_value
    return jnp.stack([real_part, imag_part], 1).astype(jnp.bfloat16)


def apply_inverse(tiles_slab, mask_slab, field, cos_value, sin_value):
    reach_blocks = OFF // 2
    extended = jnp.concatenate([rotated(field[-reach_blocks:], cos_value, -sin_value), field, rotated(field[:reach_blocks], cos_value, sin_value)], 0)
    masked = tiles_slab * mask_slab.astype(jnp.bfloat16)[:, :, None, None, None]

    def add_offset(total, offset):
        window = lax.dynamic_slice_in_dim(extended, offset, ROWBLK, 0).astype(jnp.float32)
        tile_part = lax.dynamic_index_in_dim(masked, offset, 1, keepdims=False).astype(jnp.float32)
        parts = jnp.einsum("rkab,rcbn->rkcan", tile_part, window)
        term = jnp.stack([parts[:, 0, 0] - parts[:, 1, 1], parts[:, 1, 0] + parts[:, 0, 1]], 1)
        return total + term, None

    total, _ = lax.scan(add_offset, jnp.zeros(field.shape, jnp.float32), jnp.arange(OFF, dtype=jnp.int32))
    return total


def reference(sources, inverse_tiles, pattern, phase_index):
    angle = 2.0 * jnp.pi * phase_index[0].astype(jnp.float32) / PHASES
    cos_value = jnp.cos(angle)
    sin_value = jnp.sin(angle)
    forward_fields = []
    previous = jnp.zeros(sources.shape[1:], jnp.float32)
    for slab in range(SLABS):
        field = (sources[slab].astype(jnp.float32) + coupling * previous).astype(jnp.bfloat16)
        previous = apply_inverse(inverse_tiles[slab], pattern[slab], field, cos_value, sin_value)
        forward_fields.append(previous)
    results = [None] * SLABS
    following = jnp.zeros(sources.shape[1:], jnp.float32)
    for slab in reversed(range(SLABS)):
        field = following.astype(jnp.bfloat16)
        following = forward_fields[slab] + coupling * apply_inverse(inverse_tiles[slab], pattern[slab], field, cos_value, sin_value)
        results[slab] = following
    return jnp.stack(results, 0)
```

```python
import jax
import jax.numpy as jnp
from jax import lax
from jax.sharding import PartitionSpec as P

OFF = 8
PHASES = 16
REACH = OFF // 2


coupling = 0.8


def passed_along(value, axis, by):
    length = lax.axis_size(axis)
    pairs = [(i, i + by) for i in range(length) if 0 <= i + by < length]
    return lax.ppermute(value, axis, pairs)


def folded_tiles(tiles, pattern, phase_index):
    lateral = lax.axis_size("lat")
    rows_here = tiles.shape[1]
    rows_all = rows_here * lateral
    offsets_here = tiles.shape[2]
    angle = 2.0 * jnp.pi * phase_index[0].astype(jnp.float32) / PHASES
    row = lax.axis_index("lat") * rows_here + jnp.arange(rows_here)[:, None]
    offset = lax.axis_index("col") * offsets_here + jnp.arange(offsets_here)[None, :]
    origin = row + offset - REACH
    turn = jnp.where(origin < 0, -1.0, jnp.where(origin >= rows_all, 1.0, 0.0))
    mask = pattern.astype(jnp.float32)
    cos_value = (jnp.where(turn == 0.0, 1.0, jnp.cos(angle))[None] * mask)[..., None, None]
    sin_value = ((turn * jnp.sin(angle))[None] * mask)[..., None, None]
    wide = tiles.astype(jnp.float32)
    real_part = wide[:, :, :, 0] * cos_value - wide[:, :, :, 1] * sin_value
    imag_part = wide[:, :, :, 0] * sin_value + wide[:, :, :, 1] * cos_value
    return jnp.stack([real_part, imag_part], 3).astype(jnp.bfloat16)


def shards(sources, inverse_tiles, pattern, phase_index):
    sections = lax.axis_size("sec")
    section = lax.axis_index("sec")
    slab_count = sources.shape[0]
    rows = sources.shape[1]
    place = lax.axis_index(("lat", "col"))
    rows_all = rows * lax.axis_size(("lat", "col"))
    folded = folded_tiles(inverse_tiles, pattern, phase_index)
    owned = lax.all_to_all(folded, "col", split_axis=1, concat_axis=2, tiled=True)
    first_row = place * rows - REACH
    first_row = jnp.where(first_row < 0, first_row + rows_all, first_row)

    def apply_inverse(slab, field):
        full = lax.all_gather(field, ("lat", "col"), axis=0, tiled=True)
        full = jnp.concatenate([full, full[: OFF + rows - 1]], 0)
        window = lax.dynamic_slice_in_dim(full, first_row, OFF + rows - 1, 0)
        out = []
        for row in range(rows):
            parts = jnp.einsum(
                "okab,ocbn->kcan", owned[slab, row], window[row : row + OFF],
                preferred_element_type=jnp.float32,
            )
            out.append(jnp.stack([parts[0, 0] - parts[1, 1], parts[1, 0] + parts[0, 1]], 0))
        return jnp.stack(out, 0)

    values = None
    previous = jnp.zeros(sources.shape[1:], jnp.float32)
    for turn in range(sections):
        produced = []
        for slab in range(slab_count):
            field = (sources[slab].astype(jnp.float32) + coupling * previous).astype(jnp.bfloat16)
            previous = apply_inverse(slab, field)
            produced.append(previous)
        stacked = jnp.stack(produced, 0)
        values = stacked if values is None else jnp.where(section == turn, stacked, values)
        if turn < sections - 1:
            previous = passed_along(previous.astype(jnp.bfloat16), "sec", 1).astype(jnp.float32)
    results = None
    following = None
    for turn in range(sections):
        produced = [None] * slab_count
        for slab in reversed(range(slab_count)):
            if following is None:
                updated = values[slab]
            else:
                updated = values[slab] + coupling * apply_inverse(slab, following)
            produced[slab] = updated
            following = updated.astype(jnp.bfloat16)
        stacked = jnp.stack(produced, 0)
        results = stacked if results is None else jnp.where(section == sections - 1 - turn, stacked, results)
        if turn < sections - 1:
            following = passed_along(following, "sec", -1)
    return results


def solution(mesh):
    placed = (
        P("sec", ("lat", "col"), None, None, None),
        P("sec", "lat", "col", None, None, None),
        P("sec", "lat", "col"),
        P(),
    )
    return jax.shard_map(
        shards,
        mesh=mesh,
        in_specs=placed,
        out_specs=P("sec", ("lat", "col"), None, None, None),
        check_vma=False,
    )
```

```python
import functools
import math

import jax
import jax.numpy as jnp
from jax import lax
from jax.experimental import pallas as pl
from jax.experimental.pallas import tpu as pltpu
from jax.sharding import Mesh, PartitionSpec as P

OFF = 8
PHASES = 16
REACH = OFF // 2
VMEM_BYTES = 40 * 1024 * 1024

coupling = 0.8

VMEM = pltpu.VMEM
SMEM = pltpu.SMEM


def fold_kernel(rows_all, scalars, pattern, tiles, out):
    slab = pl.program_id(0)
    row = pl.program_id(1)
    offsets = tiles.shape[2]
    blk = tiles.shape[4]
    index = lax.rem(scalars[0], PHASES)
    cos_value = jnp.float32(1.0)
    sin_value = jnp.float32(0.0)
    for step in range(1, PHASES):
        cos_value = jnp.where(index == step, jnp.float32(math.cos(2 * math.pi * step / PHASES)), cos_value)
        sin_value = jnp.where(index == step, jnp.float32(math.sin(2 * math.pi * step / PHASES)), sin_value)
    for offset in range(offsets):
        origin = scalars[1] + row + scalars[2] + offset - REACH
        below = origin < 0
        above = origin >= rows_all
        mask = pattern[slab, row, offset].astype(jnp.float32)
        real_scale = jnp.where(below | above, cos_value, 1.0) * mask
        imag_scale = jnp.where(below, -sin_value, jnp.where(above, sin_value, 0.0)) * mask
        real_part = tiles[0, 0, offset, 0].astype(jnp.float32)
        imag_part = tiles[0, 0, offset, 1].astype(jnp.float32)
        lanes = pl.ds(offset * blk, blk)
        out[0, 0, pl.ds(0, blk), lanes] = (real_part * real_scale - imag_part * imag_scale).astype(jnp.bfloat16)
        out[0, 0, pl.ds(blk, blk), lanes] = (real_part * imag_scale + imag_part * real_scale).astype(jnp.bfloat16)


def folded_tiles(tiles, pattern, phase_index, first_row, first_offset, rows_all):
    slabs, rows, offsets, _, blk, _ = tiles.shape
    scalars = jnp.stack([phase_index[0], first_row, first_offset]).astype(jnp.int32)
    return pl.pallas_call(
        functools.partial(fold_kernel, rows_all),
        grid=(slabs, rows),
        in_specs=[
            pl.BlockSpec(memory_space=SMEM),
            pl.BlockSpec(memory_space=SMEM),
            pl.BlockSpec((1, 1, offsets, 2, blk, blk), lambda s, r: (s, r, 0, 0, 0, 0)),
        ],
        out_specs=pl.BlockSpec((1, 1, 2 * blk, offsets * blk), lambda s, r: (s, r, 0, 0)),
        out_shape=jax.ShapeDtypeStruct((slabs, rows, 2 * blk, offsets * blk), jnp.bfloat16),
        compiler_params=pltpu.CompilerParams(vmem_limit_bytes=VMEM_BYTES),
    )(scalars, pattern, tiles)


def product_rows(first, full, weights):
    rows_all = full.shape[0]
    groups, rows = weights.shape[1], weights.shape[2]
    width, blk = full.shape[2], full.shape[3]
    per_group = OFF // groups
    taken = []
    for offset in range(OFF + rows - 1):
        place = lax.rem(first[0] + (offset - REACH + rows_all), rows_all)
        taken.append(full[place].reshape(2 * width, blk))
    out = []
    for row in range(rows):
        total = None
        for group in range(groups):
            start = row + group * per_group
            left = jnp.concatenate(taken[start : start + per_group], axis=1)
            part = lax.dot_general(
                left, weights[0, group, row], (((1,), (1,)), ((), ())), preferred_element_type=jnp.float32
            )
            total = part if total is None else total + part
        real_part = total[:width, :blk] - total[width:, blk:]
        imag_part = total[:width, blk:] + total[width:, :blk]
        out.append((real_part, imag_part))
    return out


def forward_kernel(first, full, weights, source, value, field):
    for row, parts in enumerate(product_rows(first, full, weights)):
        for part in range(2):
            value[row, part] = parts[part]
            following = source[row, part].astype(jnp.float32) + coupling * parts[part]
            field[row, part] = following.astype(jnp.bfloat16)


def turn_kernel(first, full, weights, value, field):
    for row, parts in enumerate(product_rows(first, full, weights)):
        for part in range(2):
            value[row, part] = parts[part]
            field[row, part] = parts[part].astype(jnp.bfloat16)


def backward_kernel(first, full, weights, value, result, field):
    for row, parts in enumerate(product_rows(first, full, weights)):
        for part in range(2):
            updated = value[row, part] + coupling * parts[part]
            result[row, part] = updated
            field[row, part] = updated.astype(jnp.bfloat16)


def applied(kernel, first, full, weights, section, extra):
    sections, groups, rows, height, depth = weights.shape
    own = (rows,) + full.shape[1:]
    whole = pl.BlockSpec(memory_space=VMEM)
    return pl.pallas_call(
        kernel,
        grid=(1,),
        in_specs=[
            pl.BlockSpec(memory_space=SMEM),
            whole,
            pl.BlockSpec((1, groups, rows, height, depth), lambda i: (section, 0, 0, 0, 0)),
        ] + [whole] * len(extra),
        out_specs=[whole, whole],
        out_shape=[jax.ShapeDtypeStruct(own, jnp.float32), jax.ShapeDtypeStruct(own, jnp.bfloat16)],
        compiler_params=pltpu.CompilerParams(vmem_limit_bytes=VMEM_BYTES),
        cost_estimate=pl.CostEstimate(
            flops=2 * rows * OFF * 4 * full.shape[2] * full.shape[3] ** 2,
            bytes_accessed=2 * groups * rows * height * depth,
            transcendentals=0,
        ),
    )(first, full, weights, *extra)


def shards(sources, inverse_tiles, pattern, phase_index):
    sections = lax.axis_size("sec")
    slabs, rows, _, blk, columns = sources.shape
    lateral, across, cores = (lax.axis_size(axis) for axis in ("lat", "cx", "core"))
    own_rows = rows * cores
    rows_all = own_rows * lateral * across
    parts = sections * cores
    width = columns // parts
    place = lax.axis_index(("lat", "cx"))
    first = (place * own_rows).reshape(1).astype(jnp.int32)

    folded = folded_tiles(
        inverse_tiles, pattern, phase_index,
        lax.axis_index("lat") * inverse_tiles.shape[1],
        lax.axis_index(("cx", "core")) * inverse_tiles.shape[2],
        rows_all,
    )
    height, depth = folded.shape[2:]
    weights = []
    for slab in range(slabs):
        piece = folded[slab].reshape(1, across, 1, own_rows, height, depth)
        piece = jnp.broadcast_to(piece, (sections, across, cores, own_rows, height, depth))
        piece = piece.reshape(sections * across * cores, own_rows, height, depth)
        piece = lax.all_to_all(piece, ("sec", "cx", "core"), 0, 0, tiled=True)
        weights.append(piece.reshape(sections, across * cores, own_rows, height, depth))

    turned = jnp.swapaxes(sources, 3, 4).reshape(slabs, rows, 2, parts, width, blk)
    turned = jnp.moveaxis(turned, 3, 0)
    turned = lax.all_to_all(turned, ("sec", "core"), 0, 0, tiled=True)
    turned = turned.reshape(sections, cores, slabs, rows, 2, width, blk)
    turned = jnp.swapaxes(turned, 1, 2).reshape(sections * slabs, own_rows, 2, width, blk)

    def gathered(field):
        return lax.all_gather(field, ("lat", "cx"), axis=0, tiled=True)

    count = sections * slabs
    values = []
    field = turned[0]
    for slab in range(count):
        tiles, section = weights[slab % slabs], slab // slabs
        if slab < count - 1:
            value, field = applied(forward_kernel, first, gathered(field), tiles, section, [turned[slab + 1]])
        else:
            value, field = applied(turn_kernel, first, gathered(field), tiles, section, [])
        values.append(value)
    results = [None] * count
    results[count - 1] = values[count - 1]
    for slab in reversed(range(count - 1)):
        tiles, section = weights[slab % slabs], slab // slabs
        results[slab], field = applied(backward_kernel, first, gathered(field), tiles, section, [values[slab]])

    stacked = jnp.stack(results, 0).reshape(sections, slabs, cores, rows, 2, width, blk)
    stacked = jnp.swapaxes(stacked, 1, 2).reshape(sections * cores, slabs, rows, 2, width, blk)
    stacked = lax.all_to_all(stacked, ("sec", "core"), 0, 0, tiled=True)
    stacked = jnp.moveaxis(stacked, 0, 3).reshape(slabs, rows, 2, columns, blk)
    return jnp.swapaxes(stacked, 3, 4)


def solution(mesh):
    sections, lateral, col = mesh.devices.shape
    fine = Mesh(mesh.devices.reshape(sections, lateral, col // 2, 2), ("sec", "lat", "cx", "core"))
    placed = (
        P("sec", ("lat", "cx", "core"), None, None, None),
        P("sec", "lat", ("cx", "core"), None, None, None),
        P("sec", "lat", ("cx", "core")),
        P(),
    )
    return jax.shard_map(
        shards,
        mesh=fine,
        in_specs=placed,
        out_specs=P("sec", ("lat", "cx", "core"), None, None, None),
        check_vma=False,
    )
```

```python
import functools
import math

import jax
import jax.numpy as jnp
from jax import lax
from jax.experimental import pallas as pl
from jax.experimental.pallas import tpu as pltpu
from jax.sharding import Mesh, PartitionSpec as P

OFF = 8
PHASES = 16
REACH = OFF // 2
VMEM_BYTES = 40 * 1024 * 1024

coupling = 0.8

VMEM = pltpu.VMEM
SMEM = pltpu.SMEM


def fold_kernel(rows_all, slab, scalars, pattern, tiles, out):
    row = pl.program_id(0)
    offsets = tiles.shape[2]
    blk = tiles.shape[4]
    index = lax.rem(scalars[0], PHASES)
    cos_value = jnp.float32(1.0)
    sin_value = jnp.float32(0.0)
    for step in range(1, PHASES):
        cos_value = jnp.where(index == step, jnp.float32(math.cos(2 * math.pi * step / PHASES)), cos_value)
        sin_value = jnp.where(index == step, jnp.float32(math.sin(2 * math.pi * step / PHASES)), sin_value)
    for offset in range(offsets):
        origin = scalars[1] + row + scalars[2] + offset - REACH
        below = origin < 0
        above = origin >= rows_all
        mask = pattern[slab, row, offset].astype(jnp.float32)
        real_scale = jnp.where(below | above, cos_value, 1.0) * mask
        imag_scale = jnp.where(below, -sin_value, jnp.where(above, sin_value, 0.0)) * mask
        real_part = tiles[0, 0, offset, 0].astype(jnp.float32)
        imag_part = tiles[0, 0, offset, 1].astype(jnp.float32)
        lanes = pl.ds(offset * blk, blk)
        upper = (real_part * real_scale - imag_part * imag_scale).astype(jnp.bfloat16)
        lower = (real_part * imag_scale + imag_part * real_scale).astype(jnp.bfloat16)
        for copy in range(out.shape[0]):
            out[copy, 0, pl.ds(0, blk), lanes] = upper
            out[copy, 0, pl.ds(blk, blk), lanes] = lower


def folded_tiles(slab, tiles, pattern, scalars, copies, rows_all):
    _, rows, offsets, _, blk, _ = tiles.shape
    return pl.pallas_call(
        functools.partial(fold_kernel, rows_all, slab),
        grid=(rows,),
        in_specs=[
            pl.BlockSpec(memory_space=SMEM),
            pl.BlockSpec(memory_space=SMEM),
            pl.BlockSpec((1, 1, offsets, 2, blk, blk), lambda r: (slab, r, 0, 0, 0, 0)),
        ],
        out_specs=pl.BlockSpec((copies, 1, 2 * blk, offsets * blk), lambda r: (0, r, 0, 0)),
        out_shape=jax.ShapeDtypeStruct((copies, rows, 2 * blk, offsets * blk), jnp.bfloat16),
        compiler_params=pltpu.CompilerParams(vmem_limit_bytes=VMEM_BYTES),
    )(scalars, pattern, tiles)


def product_rows(core, window, own_tiles, other_tiles):
    rows, width, blk = window[0].shape[0], window[0].shape[2], window[0].shape[3]
    across, per_group = own_tiles.shape[1], own_tiles.shape[4] // blk
    skip = -(-REACH // rows) * rows - REACH
    taken = []
    for offset in range(skip, skip + OFF + rows - 1):
        taken.append(window[offset // rows][offset % rows].reshape(2 * width, blk))
    first = core[0] == 0
    out = []
    for row in range(rows):
        total = None
        for cx in range(across):
            start = row + 2 * cx * per_group
            low = jnp.concatenate(taken[start : start + per_group], axis=1)
            high = jnp.concatenate(taken[start + per_group : start + 2 * per_group], axis=1)
            for left, tile in (
                (jnp.where(first, low, high), own_tiles),
                (jnp.where(first, high, low), other_tiles),
            ):
                part = lax.dot_general(
                    left, tile[0, cx, row], (((1,), (1,)), ((), ())), preferred_element_type=jnp.float32
                )
                total = part if total is None else total + part
        real_part = total[:width, :blk] - total[width:, blk:]
        imag_part = total[:width, blk:] + total[width:, :blk]
        out.append((real_part, imag_part))
    return out


def step_kernel(kind, reach, core, *refs):
    window, (own_tiles, other_tiles), rest = refs[:reach], refs[reach : reach + 2], refs[reach + 2 :]
    for row, parts in enumerate(product_rows(core, window, own_tiles, other_tiles)):
        for part in range(2):
            if kind == "forward":
                source, value, field = rest
                value[row, part] = parts[part]
                following = source[row, part].astype(jnp.float32) + coupling * parts[part]
            elif kind == "turn":
                value, field = rest
                value[row, part] = parts[part]
                following = parts[part]
            else:
                before, value, field = rest
                following = before[row, part] + coupling * parts[part]
                value[row, part] = following
            field[row, part] = following.astype(jnp.bfloat16)


def applied(kind, core, window, tiles, section, extra):
    own = window[0].shape
    whole = pl.BlockSpec(memory_space=VMEM)
    block = pl.BlockSpec((1,) + tiles[0].shape[1:], lambda i: (section, 0, 0, 0, 0))
    return pl.pallas_call(
        functools.partial(step_kernel, kind, len(window)),
        grid=(1,),
        in_specs=[pl.BlockSpec(memory_space=SMEM)] + [whole] * len(window) + [block] * 2 + [whole] * len(extra),
        out_specs=[whole, whole],
        out_shape=[jax.ShapeDtypeStruct(own, jnp.float32), jax.ShapeDtypeStruct(own, jnp.bfloat16)],
        compiler_params=pltpu.CompilerParams(vmem_limit_bytes=VMEM_BYTES),
        cost_estimate=pl.CostEstimate(
            flops=2 * own[0] * OFF * 4 * own[2] * own[3] ** 2,
            bytes_accessed=4 * math.prod(tiles[0].shape[1:]),
            transcendentals=0,
        ),
    )(core, *window, *tiles, *extra)


def shards(sources, inverse_tiles, pattern, phase_index):
    sections = lax.axis_size("sec")
    slabs, rows, _, blk, columns = sources.shape
    lateral, across, cores = (lax.axis_size(axis) for axis in ("lat", "cx", "core"))
    own_rows = rows * cores
    rows_all = own_rows * lateral * across
    parts = sections * cores
    width = columns // parts
    count = sections * slabs
    core = lax.axis_index("core").reshape(1).astype(jnp.int32)

    scalars = jnp.stack(
        [
            phase_index[0],
            lax.axis_index("lat") * inverse_tiles.shape[1],
            lax.axis_index(("cx", "core")) * inverse_tiles.shape[2],
        ]
    ).astype(jnp.int32)
    tiles = []
    for slab in range(slabs):
        folded = folded_tiles(slab, inverse_tiles, pattern, scalars, sections, rows_all)
        height, depth = folded.shape[2:]
        piece = folded.reshape(sections * across, own_rows, height, depth)
        piece = lax.all_to_all(piece, ("sec", "cx"), 0, 0, tiled=True)
        piece = piece.reshape(sections, across, own_rows, height, depth)
        tiles.append((piece, lax.ppermute(piece, "core", [(i, cores - 1 - i) for i in range(cores)])))

    turned = jnp.swapaxes(sources, 3, 4).reshape(slabs, rows, 2, parts, width, blk)
    turned = jnp.moveaxis(turned, 3, 0)
    turned = lax.all_to_all(turned, ("sec", "core"), 0, 0, tiled=True)
    turned = turned.reshape(sections, cores, slabs, rows, 2, width, blk)
    turned = jnp.swapaxes(turned, 1, 2).reshape(count, own_rows, 2, width, blk)

    ring = lateral * across
    below = -(-REACH // own_rows)
    above = -(-(OFF - 1 - REACH) // own_rows)

    def windowed(field):
        window = []
        for shift in range(-below, above + 1):
            pairs = [((i + shift) % ring, i) for i in range(ring)]
            window.append(field if shift == 0 else lax.ppermute(field, ("lat", "cx"), pairs))
        return window

    def delivered(value, other):
        both = jnp.stack([value, other], 0).reshape(sections, cores, rows, 2, width, blk)
        both = both.reshape(parts, rows, 2, width, blk)
        both = lax.all_to_all(both, ("sec", "core"), 0, 0, tiled=True)
        both = jnp.moveaxis(both, 0, 2).reshape(rows, 2, columns, blk)
        return jnp.swapaxes(both, 2, 3)

    values = []
    field = turned[0]
    for slab in range(count):
        kind, extra = ("forward", [turned[slab + 1]]) if slab < count - 1 else ("turn", [])
        value, field = applied(kind, core, windowed(field), tiles[slab % slabs], slab // slabs, extra)
        values.append(value)
    results = [None] * count
    results[count - 1] = values[count - 1]
    for slab in reversed(range(count - 1)):
        results[slab], field = applied(
            "backward", core, windowed(field), tiles[slab % slabs], slab // slabs, [values[slab]]
        )
    return jnp.stack([delivered(*results[slab::slabs]) for slab in range(slabs)], 0)


def solution(mesh):
    sections, lateral, col = mesh.devices.shape
    fine = Mesh(mesh.devices.reshape(sections, lateral, col // 2, 2), ("sec", "lat", "cx", "core"))
    placed = (
        P("sec", ("lat", "cx", "core"), None, None, None),
        P("sec", "lat", ("cx", "core"), None, None, None),
        P("sec", "lat", ("cx", "core")),
        P(),
    )
    return jax.shard_map(
        shards,
        mesh=fine,
        in_specs=placed,
        out_specs=P("sec", ("lat", "cx", "core"), None, None, None),
        check_vma=False,
    )
```

```python
import functools
import math

import jax
import jax.numpy as jnp
from jax import lax
from jax.experimental import pallas as pl
from jax.experimental.pallas import tpu as pltpu
from jax.sharding import Mesh, PartitionSpec as P

OFF = 8
PHASES = 16
REACH = OFF // 2
VMEM_BYTES = 40 * 1024 * 1024

coupling = 0.8

VMEM = pltpu.VMEM
SMEM = pltpu.SMEM
WHOLE = pl.BlockSpec(memory_space=VMEM)
SCALARS = pl.BlockSpec(memory_space=SMEM)


def fold_kernel(rows_all, slab, scalars, pattern, tiles, out):
    row = pl.program_id(0)
    offsets = tiles.shape[2]
    blk = tiles.shape[4]
    index = lax.rem(scalars[0], PHASES)
    cos_value = jnp.float32(1.0)
    sin_value = jnp.float32(0.0)
    for step in range(1, PHASES):
        cos_value = jnp.where(index == step, jnp.float32(math.cos(2 * math.pi * step / PHASES)), cos_value)
        sin_value = jnp.where(index == step, jnp.float32(math.sin(2 * math.pi * step / PHASES)), sin_value)
    for offset in range(offsets):
        origin = scalars[1] + row + scalars[2] + offset - REACH
        below = origin < 0
        above = origin >= rows_all
        mask = pattern[slab, row, offset].astype(jnp.float32)
        real_scale = jnp.where(below | above, cos_value, 1.0) * mask
        imag_scale = jnp.where(below, -sin_value, jnp.where(above, sin_value, 0.0)) * mask
        real_part = tiles[0, 0, offset, 0].astype(jnp.float32)
        imag_part = tiles[0, 0, offset, 1].astype(jnp.float32)
        lanes = pl.ds(offset * blk, blk)
        out[0, pl.ds(0, blk), lanes] = (real_part * real_scale - imag_part * imag_scale).astype(jnp.bfloat16)
        out[0, pl.ds(blk, blk), lanes] = (real_part * imag_scale + imag_part * real_scale).astype(jnp.bfloat16)


def folded_tiles(slab, tiles, pattern, scalars, rows_all):
    _, rows, offsets, _, blk, _ = tiles.shape
    return pl.pallas_call(
        functools.partial(fold_kernel, rows_all, slab),
        grid=(rows,),
        in_specs=[
            SCALARS,
            SCALARS,
            pl.BlockSpec((1, 1, offsets, 2, blk, blk), lambda r: (slab, r, 0, 0, 0, 0)),
        ],
        out_specs=pl.BlockSpec((1, 2 * blk, offsets * blk), lambda r: (r, 0, 0)),
        out_shape=jax.ShapeDtypeStruct((rows, 2 * blk, offsets * blk), jnp.bfloat16),
        compiler_params=pltpu.CompilerParams(vmem_limit_bytes=VMEM_BYTES),
    )(scalars, pattern, tiles)


def step_kernel(kind, reach, pieces, groups, *refs):
    window, weights, rest, taken = refs[:reach], refs[reach : reach + pieces], refs[reach + pieces : -1], refs[-1]
    rows, _, width, blk = window[0].shape
    per_group = weights[0].shape[2] // blk
    skip = -(-REACH // rows) * rows - REACH
    for place in range(OFF + rows - 1):
        taken[place] = window[(place + skip) // rows][(place + skip) % rows].reshape(2 * width, blk)
    for row in range(rows):
        total = None
        for piece in range(pieces):
            start = row + groups[piece] * per_group
            left = jnp.concatenate([taken[start + offset] for offset in range(per_group)], axis=1)
            part = lax.dot_general(
                left, weights[piece][row], (((1,), (1,)), ((), ())), preferred_element_type=jnp.float32
            )
            total = part if total is None else total + part
        product = (total[:width, :blk] - total[width:, blk:], total[:width, blk:] + total[width:, :blk])
        for part in range(2):
            extra = list(rest)
            value = product[part]
            if "add" in kind:
                value = extra.pop(0)[row, part] + coupling * value
            following = value
            if "source" in kind:
                following = extra.pop(0)[row, part].astype(jnp.float32) + coupling * value
            extra.pop(0)[row, part] = value
            if "last" not in kind:
                extra.pop(0)[row, part] = following.astype(jnp.bfloat16)


def kernel_of(kind, reach, pieces, groups, *refs):
    step_kernel(kind, reach, pieces, [groups[piece] for piece in range(pieces)], *refs)


def applied(kind, groups, window, weights, extra):
    own = window[0].shape
    rows, height, depth = weights[0].shape
    out_shape = [jax.ShapeDtypeStruct(own, jnp.float32)]
    if "last" not in kind:
        out_shape.append(jax.ShapeDtypeStruct(own, jnp.bfloat16))

    def body(groups_ref, *refs):
        kernel_of(kind, len(window), len(weights), groups_ref, *refs)

    return pl.pallas_call(
        body,
        in_specs=[SCALARS] + [WHOLE] * (len(window) + len(weights) + len(extra)),
        out_specs=[WHOLE] * len(out_shape),
        out_shape=out_shape,
        scratch_shapes=[VMEM((OFF + rows - 1, 2 * own[2], own[3]), jnp.bfloat16)],
        compiler_params=pltpu.CompilerParams(vmem_limit_bytes=VMEM_BYTES),
        cost_estimate=pl.CostEstimate(
            flops=2 * own[0] * OFF * 4 * own[2] * own[3] ** 2,
            bytes_accessed=2 * len(weights) * rows * height * depth,
            transcendentals=0,
        ),
    )(groups, *window, *weights, *extra)


def shifted(value, axis, by):
    size = lax.axis_size(axis)
    return lax.ppermute(value, axis, [((i - by) % size, i) for i in range(size)])


def exchanged(folded):
    across, cores = lax.axis_size("cx"), lax.axis_size("core")
    pieces = []
    for by_cx in range(across):
        piece = shifted(folded, "cx", by_cx) if by_cx else folded
        pieces += [shifted(piece, "core", by_core) if by_core else piece for by_core in range(cores)]
    return pieces


def shards(sources, inverse_tiles, pattern, phase_index):
    sections = lax.axis_size("sec")
    section = lax.axis_index("sec")
    slabs, rows, _, blk, columns = sources.shape
    lateral, across, cores = (lax.axis_size(axis) for axis in ("lat", "cx", "core"))
    cx, core = lax.axis_index("cx"), lax.axis_index("core")
    parts = across * cores
    tile_rows = rows * parts
    width = columns // parts
    groups = jnp.stack(
        [
            lax.rem(cx + (across - by_cx), across) * cores + lax.rem(core + (cores - by_core), cores)
            for by_cx in range(across)
            for by_core in range(cores)
        ]
    ).astype(jnp.int32)
    scalars = jnp.stack(
        [
            phase_index[0],
            lax.axis_index("lat") * tile_rows,
            lax.axis_index(("cx", "core")) * inverse_tiles.shape[2],
        ]
    ).astype(jnp.int32)
    tiles = []
    for slab in range(slabs):
        folded = folded_tiles(slab, inverse_tiles, pattern, scalars, lateral * tile_rows)
        tiles.append(exchanged(folded))

    turned = jnp.swapaxes(sources, 3, 4).reshape(slabs, rows, 2, parts, width, blk)
    turned = jnp.moveaxis(turned, 3, 0)
    turned = lax.all_to_all(turned, ("cx", "core"), 0, 0, tiled=True)
    turned = jnp.swapaxes(turned, 0, 1).reshape(slabs, tile_rows, 2, width, blk)

    below = -(-REACH // tile_rows)
    above = -(-(OFF - 1 - REACH) // tile_rows)

    def windowed(field, by=0):
        window = []
        for shift in range(-below, above + 1):
            pairs = []
            for sec in range(sections):
                if 0 <= sec - by < sections:
                    pairs += [
                        ((sec - by) * lateral + (lat + shift) % lateral, sec * lateral + lat) for lat in range(lateral)
                    ]
            moves = by != 0 or shift != 0
            window.append(lax.ppermute(field, ("sec", "lat"), pairs) if moves else field)
        return window

    def delivered(value):
        whole = value.reshape(parts, rows, 2, width, blk)
        whole = lax.all_to_all(whole, ("cx", "core"), 0, 0, tiled=True)
        whole = jnp.moveaxis(whole, 0, 2).reshape(rows, 2, columns, blk)
        return jnp.swapaxes(whole, 2, 3)

    values = []
    window = windowed(turned[0])
    for turn in range(sections):
        values.append([])
        for slab in range(slabs):
            kind, extra = [], []
            if turn > 0 and slab == 0:
                kind.append("add")
                extra.append(values[0][0])
            if slab < slabs - 1:
                kind.append("source")
                extra.append(turned[slab + 1])
            value, field = applied(kind, groups, window, tiles[slab], extra)
            values[turn].append(value)
            last = turn == sections - 1 and slab == slabs - 1
            window = windowed(field, 1 if slab == slabs - 1 and not last else 0)
    results = [None] * slabs
    for turn in range(sections):
        owner = sections - 1 - turn
        for slab in reversed(range(slabs)):
            if turn == 0 and slab == slabs - 1:
                results[slab] = values[owner][slab]
                continue
            last = turn == sections - 1 and slab == 0
            updated = applied(["add"] + ["last"] * last, groups, window, tiles[slab], [values[owner][slab]])
            results[slab] = updated[0] if turn == 0 else jnp.where(section == owner, updated[0], results[slab])
            if not last:
                window = windowed(updated[1], -1 if slab == 0 else 0)
    return jnp.stack([delivered(result) for result in results], 0)


def solution(mesh):
    sections, lateral, col = mesh.devices.shape
    fine = Mesh(mesh.devices.reshape(sections, lateral, col // 2, 2), ("sec", "lat", "cx", "core"))
    placed = (
        P("sec", ("lat", "cx", "core"), None, None, None),
        P("sec", "lat", ("cx", "core"), None, None, None),
        P("sec", "lat", ("cx", "core")),
        P(),
    )
    return jax.shard_map(
        shards,
        mesh=fine,
        in_specs=placed,
        out_specs=P("sec", ("lat", "cx", "core"), None, None, None),
        check_vma=False,
    )
```

```python
import functools
import math

import jax
import jax.numpy as jnp
from jax import lax
from jax.experimental import pallas as pl
from jax.experimental.pallas import tpu as pltpu
from jax.sharding import Mesh, PartitionSpec as P

OFF = 8
PHASES = 16
REACH = OFF // 2
VMEM_BYTES = 12 * 1024 * 1024

coupling = 0.8

VMEM = pltpu.VMEM
SMEM = pltpu.SMEM
WHOLE = pl.BlockSpec(memory_space=VMEM)
SCALARS = pl.BlockSpec(memory_space=SMEM)


def fold_kernel(rows_all, slab, scalars, pattern, tiles, out):
    row = pl.program_id(0)
    offsets = tiles.shape[2]
    blk = tiles.shape[4]
    index = lax.rem(scalars[0], PHASES)
    cos_value = jnp.float32(1.0)
    sin_value = jnp.float32(0.0)
    for step in range(1, PHASES):
        cos_value = jnp.where(index == step, jnp.float32(math.cos(2 * math.pi * step / PHASES)), cos_value)
        sin_value = jnp.where(index == step, jnp.float32(math.sin(2 * math.pi * step / PHASES)), sin_value)
    for offset in range(offsets):
        origin = scalars[1] + row + scalars[2] + offset - REACH
        below = origin < 0
        above = origin >= rows_all
        mask = pattern[slab, row, offset].astype(jnp.float32)
        real_scale = jnp.where(below | above, cos_value, 1.0) * mask
        imag_scale = jnp.where(below, -sin_value, jnp.where(above, sin_value, 0.0)) * mask
        real_part = tiles[0, 0, offset, 0].astype(jnp.float32)
        imag_part = tiles[0, 0, offset, 1].astype(jnp.float32)
        lanes = pl.ds(offset * blk, blk)
        out[0, pl.ds(0, blk), lanes] = (real_part * real_scale - imag_part * imag_scale).astype(jnp.bfloat16)
        out[0, pl.ds(blk, blk), lanes] = (real_part * imag_scale + imag_part * real_scale).astype(jnp.bfloat16)


def folded_tiles(slab, tiles, pattern, scalars, rows_all):
    _, rows, offsets, _, blk, _ = tiles.shape
    return pl.pallas_call(
        functools.partial(fold_kernel, rows_all, slab),
        grid=(rows,),
        in_specs=[
            SCALARS,
            SCALARS,
            pl.BlockSpec((1, 1, offsets, 2, blk, blk), lambda r: (slab, r, 0, 0, 0, 0)),
        ],
        out_specs=pl.BlockSpec((1, 2 * blk, offsets * blk), lambda r: (r, 0, 0)),
        out_shape=jax.ShapeDtypeStruct((rows, 2 * blk, offsets * blk), jnp.bfloat16),
        compiler_params=pltpu.CompilerParams(vmem_limit_bytes=VMEM_BYTES),
    )(scalars, pattern, tiles)


def step_kernel(kind, reach, pieces, scalars, *refs):
    window, weights, rest, taken = refs[:reach], refs[reach : reach + pieces], refs[reach + pieces : -1], refs[-1]
    rows, _, width, blk = window[0].shape
    per_group = weights[0].shape[2] // blk
    skip = -(-REACH // rows) * rows - REACH
    for place in range(OFF + rows - 1):
        taken[place] = window[(place + skip) // rows][(place + skip) % rows].reshape(2 * width, blk)
    starts = [scalars[2 + piece] * per_group for piece in range(pieces)]
    for row in range(rows):
        total = None
        for piece in range(pieces):
            left = jnp.concatenate([taken[starts[piece] + (row + offset)] for offset in range(per_group)], axis=1)
            part = lax.dot_general(
                left, weights[piece][row], (((1,), (1,)), ((), ())), preferred_element_type=jnp.float32
            )
            total = part if total is None else total + part
        product = (total[:width, :blk] - total[width:, blk:], total[:width, blk:] + total[width:, :blk])
        for part in range(2):
            extra = list(rest)
            value = product[part]
            if "add" in kind:
                value = extra.pop(0)[row, part] + coupling * value
            following = value
            if "source" in kind:
                following = extra.pop(0)[row, part].astype(jnp.float32) + coupling * value
            if "merge" in kind:
                value = jnp.where(scalars[0] == kind["merge"], value, extra.pop(0)[row, part])
            if "pieces" in kind:
                for goal in range(kind["pieces"]):
                    extra.pop(0)
                each = rows // kind["pieces"]
                shift = lax.rem(row // each - scalars[1] + kind["pieces"], kind["pieces"])
                for by in range(kind["pieces"]):
                    sent = rest[len(rest) - len(extra) - kind["pieces"] + by]

                    @pl.when(shift == by)
                    def _():
                        sent[row % each, part] = value
            else:
                extra.pop(0)[row, part] = value
            if "last" not in kind:
                extra.pop(0)[row, part] = following.astype(jnp.bfloat16)


def applied(kind, scalars, window, weights, extra):
    own = window[0].shape
    rows, height, depth = weights[0].shape
    if "pieces" in kind:
        count = kind["pieces"]
        out_shape = [jax.ShapeDtypeStruct((own[0] // count,) + own[1:], jnp.float32)] * count
    else:
        out_shape = [jax.ShapeDtypeStruct(own, jnp.float32)]
    if "last" not in kind:
        out_shape.append(jax.ShapeDtypeStruct(own, jnp.bfloat16))
    return pl.pallas_call(
        functools.partial(step_kernel, kind, len(window), len(weights)),
        in_specs=[SCALARS] + [WHOLE] * (len(window) + len(weights) + len(extra)),
        out_specs=[WHOLE] * len(out_shape),
        out_shape=out_shape,
        scratch_shapes=[VMEM((OFF + rows - 1, 2 * own[2], own[3]), jnp.bfloat16)],
        compiler_params=pltpu.CompilerParams(vmem_limit_bytes=VMEM_BYTES),
        cost_estimate=pl.CostEstimate(
            flops=2 * own[0] * OFF * 4 * own[2] * own[3] ** 2,
            bytes_accessed=2 * len(weights) * rows * height * depth,
            transcendentals=0,
        ),
    )(scalars, *window, *weights, *extra)


def assembling_kernel(slabs, scalars, *refs):
    pieces, out, held = refs[:-2], refs[-2], refs[-1]
    count = len(pieces) // slabs
    rows = pieces[0].shape[0]
    for slab in range(slabs):
        for by in range(count):
            held[slab, lax.rem(scalars[1] - by + count, count)] = pieces[slab * count + by][...]
    for slab in range(slabs):
        for row in range(rows):
            for part in range(2):
                whole = jnp.concatenate([held[slab, place, row, part] for place in range(count)], axis=0)
                out[slab, row, part] = whole.T


def assembled(scalars, pieces):
    slabs, count = len(pieces), len(pieces[0])
    rows, _, width, blk = pieces[0][0].shape
    return pl.pallas_call(
        functools.partial(assembling_kernel, slabs),
        in_specs=[SCALARS] + [WHOLE] * (slabs * count),
        out_specs=WHOLE,
        out_shape=jax.ShapeDtypeStruct((slabs, rows, 2, blk, width * count), jnp.float32),
        scratch_shapes=[VMEM((slabs, count, rows, 2, width, blk), jnp.float32)],
        compiler_params=pltpu.CompilerParams(vmem_limit_bytes=VMEM_BYTES),
    )(scalars, *[piece for slab in pieces for piece in slab])


def shifted(value, axis, by):
    size = lax.axis_size(axis)
    return lax.ppermute(value, axis, [((i - by) % size, i) for i in range(size)])


def shards(sources, inverse_tiles, pattern, phase_index):
    sections = lax.axis_size("sec")
    section = lax.axis_index("sec")
    slabs, rows, _, blk, columns = sources.shape
    lateral, across, cores = (lax.axis_size(axis) for axis in ("lat", "cx", "core"))
    cx, core = lax.axis_index("cx"), lax.axis_index("core")
    parts = across * cores
    tile_rows = rows * parts
    width = columns // parts
    scalars = jnp.stack(
        [section, cx * cores + core]
        + [
            lax.rem(cx + (across - by_cx), across) * cores + lax.rem(core + (cores - by_core), cores)
            for by_cx in range(across)
            for by_core in range(cores)
        ]
    ).astype(jnp.int32)
    fold_scalars = jnp.stack(
        [
            phase_index[0],
            lax.axis_index("lat") * tile_rows,
            lax.axis_index(("cx", "core")) * inverse_tiles.shape[2],
        ]
    ).astype(jnp.int32)

    below = -(-REACH // tile_rows)
    above = -(-(OFF - 1 - REACH) // tile_rows)

    def windowed(field, by=0):
        window = []
        for shift in range(-below, above + 1):
            pairs = []
            for sec in range(sections):
                if 0 <= sec - by < sections:
                    pairs += [
                        ((sec - by) * lateral + (lat + shift) % lateral, sec * lateral + lat) for lat in range(lateral)
                    ]
            moves = by != 0 or shift != 0
            window.append(lax.ppermute(field, ("sec", "lat"), pairs) if moves else field)
        return window

    turned = jnp.swapaxes(sources, 3, 4).reshape(slabs, rows, 2, parts, width, blk)
    turned = jnp.moveaxis(turned, 3, 0)
    turned = lax.all_to_all(turned, ("cx", "core"), 0, 0, tiled=True)
    turned = jnp.swapaxes(turned, 0, 1).reshape(slabs, tile_rows, 2, width, blk)
    window = windowed(turned[0])

    tiles = []
    for slab in range(slabs):
        folded = folded_tiles(slab, inverse_tiles, pattern, fold_scalars, lateral * tile_rows)
        near = [shifted(folded, "cx", by_cx) if by_cx else folded for by_cx in range(across)]
        if slab == 0:
            window, near[1:] = lax.optimization_barrier((window, near[1:]))
        tiles.append(
            [shifted(piece, "core", by_core) if by_core else piece for piece in near for by_core in range(cores)]
        )

    def delivered(pieces):
        received = []
        for by, piece in enumerate(pieces):
            pairs = [(place, (place + by) % parts) for place in range(parts)]
            received.append(lax.ppermute(piece, ("cx", "core"), pairs) if by else piece)
        return received

    values = []
    for turn in range(sections):
        values.append([])
        for slab in range(slabs):
            kind, extra = {}, []
            if turn > 0 and slab == 0:
                kind["add"] = True
                extra.append(values[0][0])
            if slab < slabs - 1:
                kind["source"] = True
                extra.append(turned[slab + 1])
            value, field = applied(kind, scalars, window, tiles[slab], extra)
            values[turn].append(value)
            last = turn == sections - 1 and slab == slabs - 1
            window = windowed(field, 1 if slab == slabs - 1 and not last else 0)
    results = [None] * slabs
    for turn in range(sections):
        owner = sections - 1 - turn
        for slab in reversed(range(slabs)):
            if turn == 0 and slab == slabs - 1:
                results[slab] = values[owner][slab]
                continue
            kind, extra = {"add": True}, [values[owner][slab]]
            if turn > 0:
                kind["merge"] = owner
                extra.append(results[slab])
            if turn == sections - 1:
                kind["pieces"] = parts
                if slab == 0:
                    kind["last"] = True
            updated = applied(kind, scalars, window, tiles[slab], extra)
            if turn == sections - 1:
                results[slab] = delivered(updated[:parts])
            else:
                results[slab] = updated[0]
            if "last" not in kind:
                window = windowed(updated[-1], -1 if slab == 0 else 0)
    return assembled(scalars, results)


def solution(mesh):
    sections, lateral, col = mesh.devices.shape
    fine = Mesh(mesh.devices.reshape(sections, lateral, col // 2, 2), ("sec", "lat", "cx", "core"))
    placed = (
        P("sec", ("lat", "cx", "core"), None, None, None),
        P("sec", "lat", ("cx", "core"), None, None, None),
        P("sec", "lat", ("cx", "core")),
        P(),
    )
    return jax.shard_map(
        shards,
        mesh=fine,
        in_specs=placed,
        out_specs=P("sec", ("lat", "cx", "core"), None, None, None),
        check_vma=False,
    )
```

```python
import functools
import math

import jax
import jax.numpy as jnp
from jax import lax
from jax.experimental import pallas as pl
from jax.experimental.pallas import tpu as pltpu
from jax.sharding import Mesh, PartitionSpec as P

OFF = 8
PHASES = 16
REACH = OFF // 2
VMEM_BYTES = 12 * 1024 * 1024

coupling = 0.8

VMEM = pltpu.VMEM
SMEM = pltpu.SMEM
WHOLE = pl.BlockSpec(memory_space=VMEM)
SCALARS = pl.BlockSpec(memory_space=SMEM)


def fold_kernel(rows_all, slab, scalars, pattern, tiles, out):
    row = pl.program_id(0)
    offsets = tiles.shape[2]
    blk = tiles.shape[4]
    index = lax.rem(scalars[0], PHASES)
    cos_value = jnp.float32(1.0)
    sin_value = jnp.float32(0.0)
    for step in range(1, PHASES):
        cos_value = jnp.where(index == step, jnp.float32(math.cos(2 * math.pi * step / PHASES)), cos_value)
        sin_value = jnp.where(index == step, jnp.float32(math.sin(2 * math.pi * step / PHASES)), sin_value)
    for offset in range(offsets):
        origin = scalars[1] + row + scalars[2] + offset - REACH
        below = origin < 0
        above = origin >= rows_all
        mask = pattern[slab, row, offset].astype(jnp.float32)
        real_scale = jnp.where(below | above, cos_value, 1.0) * mask
        imag_scale = jnp.where(below, -sin_value, jnp.where(above, sin_value, 0.0)) * mask
        real_part = tiles[0, 0, offset, 0].astype(jnp.float32)
        imag_part = tiles[0, 0, offset, 1].astype(jnp.float32)
        lanes = pl.ds(offset * blk, blk)
        out[0, pl.ds(0, blk), lanes] = (real_part * real_scale - imag_part * imag_scale).astype(jnp.bfloat16)
        out[0, pl.ds(blk, blk), lanes] = (real_part * imag_scale + imag_part * real_scale).astype(jnp.bfloat16)


def folded_tiles(slab, tiles, pattern, scalars, rows_all):
    _, rows, offsets, _, blk, _ = tiles.shape
    return pl.pallas_call(
        functools.partial(fold_kernel, rows_all, slab),
        grid=(rows,),
        in_specs=[
            SCALARS,
            SCALARS,
            pl.BlockSpec((1, 1, offsets, 2, blk, blk), lambda r: (slab, r, 0, 0, 0, 0)),
        ],
        out_specs=pl.BlockSpec((1, 2 * blk, offsets * blk), lambda r: (r, 0, 0)),
        out_shape=jax.ShapeDtypeStruct((rows, 2 * blk, offsets * blk), jnp.bfloat16),
        compiler_params=pltpu.CompilerParams(vmem_limit_bytes=VMEM_BYTES),
    )(scalars, pattern, tiles)


def step_kernel(kind, reach, pieces, scalars, *refs):
    window, weights, rest = refs[:reach], refs[reach : reach + pieces], refs[reach + pieces : -2]
    taken, held = refs[-2:]
    rows, _, width, blk = window[0].shape
    per_group = weights[0].shape[2] // blk
    skip = -(-REACH // rows) * rows - REACH
    for place in range(OFF + rows - 1):
        taken[place] = window[(place + skip) // rows][(place + skip) % rows].reshape(2 * width, blk)
    starts = [scalars[2 + piece] * per_group for piece in range(pieces)]
    for row in range(rows):
        total = None
        for piece in range(pieces):
            left = jnp.concatenate([taken[starts[piece] + (row + offset)] for offset in range(per_group)], axis=1)
            part = lax.dot_general(
                left, weights[piece][row], (((1,), (1,)), ((), ())), preferred_element_type=jnp.float32
            )
            total = part if total is None else total + part
        product = (total[:width, :blk] - total[width:, blk:], total[:width, blk:] + total[width:, :blk])
        for part in range(2):
            extra = list(rest)
            value = product[part]
            if "add" in kind:
                value = extra.pop(0)[row, part] + coupling * value
            following = value
            if "source" in kind:
                following = extra.pop(0)[row, part].astype(jnp.float32) + coupling * value
            if "merge" in kind:
                value = jnp.where(scalars[0] == kind["merge"], value, extra.pop(0)[row, part])
            if "pieces" in kind:
                held[row, part] = value
                del extra[: kind["pieces"]]
            else:
                extra.pop(0)[row, part] = value
            if "last" not in kind:
                extra.pop(0)[row, part] = following.astype(jnp.bfloat16)
    if "pieces" in kind:
        each = rows // kind["pieces"]
        for by in range(kind["pieces"]):
            goal = lax.rem(scalars[1] + by, kind["pieces"]) * each
            for row in range(each):
                rest[kind["inputs"] + by][row] = held[goal + row]


def applied(kind, scalars, window, weights, extra):
    own = window[0].shape
    rows, height, depth = weights[0].shape
    if "pieces" in kind:
        count = kind["pieces"]
        out_shape = [jax.ShapeDtypeStruct((own[0] // count,) + own[1:], jnp.float32)] * count
    else:
        out_shape = [jax.ShapeDtypeStruct(own, jnp.float32)]
    if "last" not in kind:
        out_shape.append(jax.ShapeDtypeStruct(own, jnp.bfloat16))
    return pl.pallas_call(
        functools.partial(step_kernel, kind | {"inputs": len(extra)}, len(window), len(weights)),
        in_specs=[SCALARS] + [WHOLE] * (len(window) + len(weights) + len(extra)),
        out_specs=[WHOLE] * len(out_shape),
        out_shape=out_shape,
        scratch_shapes=[VMEM((OFF + rows - 1, 2 * own[2], own[3]), jnp.bfloat16), VMEM(own, jnp.float32)],
        compiler_params=pltpu.CompilerParams(vmem_limit_bytes=VMEM_BYTES),
        cost_estimate=pl.CostEstimate(
            flops=2 * own[0] * OFF * 4 * own[2] * own[3] ** 2,
            bytes_accessed=2 * len(weights) * rows * height * depth,
            transcendentals=0,
        ),
    )(scalars, *window, *weights, *extra)


def assembling_kernel(slabs, scalars, *refs):
    pieces, out, held = refs[:-2], refs[-2], refs[-1]
    count = len(pieces) // slabs
    rows = pieces[0].shape[0]
    for slab in range(slabs):
        for by in range(count):
            held[slab, lax.rem(scalars[1] - by + count, count)] = pieces[slab * count + by][...]
    for slab in range(slabs):
        for row in range(rows):
            for part in range(2):
                whole = jnp.concatenate([held[slab, place, row, part] for place in range(count)], axis=0)
                out[slab, row, part] = whole.T


def assembled(scalars, pieces):
    slabs, count = len(pieces), len(pieces[0])
    rows, _, width, blk = pieces[0][0].shape
    return pl.pallas_call(
        functools.partial(assembling_kernel, slabs),
        in_specs=[SCALARS] + [WHOLE] * (slabs * count),
        out_specs=WHOLE,
        out_shape=jax.ShapeDtypeStruct((slabs, rows, 2, blk, width * count), jnp.float32),
        scratch_shapes=[VMEM((slabs, count, rows, 2, width, blk), jnp.float32)],
        compiler_params=pltpu.CompilerParams(vmem_limit_bytes=VMEM_BYTES),
    )(scalars, *[piece for slab in pieces for piece in slab])


def shifted(value, axis, by):
    size = lax.axis_size(axis)
    return lax.ppermute(value, axis, [((i - by) % size, i) for i in range(size)])


def shards(sources, inverse_tiles, pattern, phase_index):
    sections = lax.axis_size("sec")
    section = lax.axis_index("sec")
    slabs, rows, _, blk, columns = sources.shape
    lateral, across, cores = (lax.axis_size(axis) for axis in ("lat", "cx", "core"))
    cx, core = lax.axis_index("cx"), lax.axis_index("core")
    parts = across * cores
    tile_rows = rows * parts
    width = columns // parts
    scalars = jnp.stack(
        [section, cx * cores + core]
        + [
            lax.rem(cx + (across - by_cx), across) * cores + lax.rem(core + (cores - by_core), cores)
            for by_cx in range(across)
            for by_core in range(cores)
        ]
    ).astype(jnp.int32)
    fold_scalars = jnp.stack(
        [
            phase_index[0],
            lax.axis_index("lat") * tile_rows,
            lax.axis_index(("cx", "core")) * inverse_tiles.shape[2],
        ]
    ).astype(jnp.int32)

    below = -(-REACH // tile_rows)
    above = -(-(OFF - 1 - REACH) // tile_rows)

    def windowed(field, by=0):
        if by:
            pairs = [(sec - by, sec) for sec in range(sections) if 0 <= sec - by < sections]
            field = lax.ppermute(field, "sec", pairs)
        return [shifted(field, "lat", -shift) if shift else field for shift in range(-below, above + 1)]

    tiles = []
    folded = [
        folded_tiles(slab, inverse_tiles, pattern, fold_scalars, lateral * tile_rows) for slab in range(slabs)
    ]

    turned = jnp.swapaxes(sources, 3, 4).reshape(slabs, rows, 2, parts, width, blk)
    around = jnp.stack(windowed(turned[0]) + [turned[slab] for slab in range(1, slabs)], 0)
    around = lax.all_to_all(jnp.moveaxis(around, 3, 0), ("cx", "core"), 0, 0, tiled=True)
    around = jnp.swapaxes(around, 0, 1).reshape(-1, tile_rows, 2, width, blk)
    window = [around[place] for place in range(below + above + 1)]
    turned = [None] + [around[below + above + slab] for slab in range(1, slabs)]

    for slab in range(slabs):
        if slab == 1:
            window, folded[1:] = lax.optimization_barrier((window, folded[1:]))
        near = [shifted(folded[slab], "cx", by_cx) if by_cx else folded[slab] for by_cx in range(across)]
        tiles.append(
            [shifted(piece, "core", by_core) if by_core else piece for piece in near for by_core in range(cores)]
        )

    def delivered(pieces):
        received = []
        for by, piece in enumerate(pieces):
            pairs = [(place, (place + by) % parts) for place in range(parts)]
            received.append(lax.ppermute(piece, ("cx", "core"), pairs) if by else piece)
        return received

    values = []
    for turn in range(sections):
        values.append([])
        for slab in range(slabs):
            kind, extra = {}, []
            if turn > 0 and slab == 0:
                kind["add"] = True
                extra.append(values[0][0])
            if slab < slabs - 1:
                kind["source"] = True
                extra.append(turned[slab + 1])
            value, field = applied(kind, scalars, window, tiles[slab], extra)
            values[turn].append(value)
            last = turn == sections - 1 and slab == slabs - 1
            window = windowed(field, 1 if slab == slabs - 1 and not last else 0)
    results = [None] * slabs
    for turn in range(sections):
        owner = sections - 1 - turn
        for slab in reversed(range(slabs)):
            if turn == 0 and slab == slabs - 1:
                results[slab] = values[owner][slab]
                continue
            kind, extra = {"add": True}, [values[owner][slab]]
            if turn > 0:
                kind["merge"] = owner
                extra.append(results[slab])
            if turn == sections - 1:
                kind["pieces"] = parts
                if slab == 0:
                    kind["last"] = True
            updated = applied(kind, scalars, window, tiles[slab], extra)
            if turn == sections - 1:
                results[slab] = delivered(updated[:parts])
            else:
                results[slab] = updated[0]
            if "last" not in kind:
                window = windowed(updated[-1], -1 if slab == 0 else 0)
    return assembled(scalars, results)


def solution(mesh):
    sections, lateral, col = mesh.devices.shape
    fine = Mesh(mesh.devices.reshape(sections, lateral, col // 2, 2), ("sec", "lat", "cx", "core"))
    placed = (
        P("sec", ("lat", "cx", "core"), None, None, None),
        P("sec", "lat", ("cx", "core"), None, None, None),
        P("sec", "lat", ("cx", "core")),
        P(),
    )
    return jax.shard_map(
        shards,
        mesh=fine,
        in_specs=placed,
        out_specs=P("sec", ("lat", "cx", "core"), None, None, None),
        check_vma=False,
    )
```

```python
import functools
import math

import jax
import jax.numpy as jnp
from jax import lax
from jax.experimental import pallas as pl
from jax.experimental.pallas import tpu as pltpu
from jax.sharding import Mesh, PartitionSpec as P

OFF = 8
PHASES = 16
REACH = OFF // 2
VMEM_BYTES = 12 * 1024 * 1024

coupling = 0.8

VMEM = pltpu.VMEM
SMEM = pltpu.SMEM
WHOLE = pl.BlockSpec(memory_space=VMEM)
SCALARS = pl.BlockSpec(memory_space=SMEM)


def fold_kernel(rows_all, slab, scalars, pattern, tiles, out):
    row = pl.program_id(0)
    offsets = tiles.shape[2]
    blk = tiles.shape[4]
    index = lax.rem(scalars[0], PHASES)
    cos_value = jnp.float32(1.0)
    sin_value = jnp.float32(0.0)
    for step in range(1, PHASES):
        cos_value = jnp.where(index == step, jnp.float32(math.cos(2 * math.pi * step / PHASES)), cos_value)
        sin_value = jnp.where(index == step, jnp.float32(math.sin(2 * math.pi * step / PHASES)), sin_value)
    for offset in range(offsets):
        origin = scalars[1] + row + scalars[2] + offset - REACH
        below = origin < 0
        above = origin >= rows_all
        mask = pattern[slab, row, offset].astype(jnp.float32)
        real_scale = jnp.where(below | above, cos_value, 1.0) * mask
        imag_scale = jnp.where(below, -sin_value, jnp.where(above, sin_value, 0.0)) * mask
        real_part = tiles[0, 0, offset, 0].astype(jnp.float32)
        imag_part = tiles[0, 0, offset, 1].astype(jnp.float32)
        lanes = pl.ds(offset * blk, blk)
        out[0, pl.ds(0, blk), lanes] = (real_part * real_scale - imag_part * imag_scale).astype(jnp.bfloat16)
        out[0, pl.ds(blk, blk), lanes] = (real_part * imag_scale + imag_part * real_scale).astype(jnp.bfloat16)


def folded_tiles(slab, tiles, pattern, scalars, rows_all):
    _, rows, offsets, _, blk, _ = tiles.shape
    return pl.pallas_call(
        functools.partial(fold_kernel, rows_all, slab),
        grid=(rows,),
        in_specs=[
            SCALARS,
            SCALARS,
            pl.BlockSpec((1, 1, offsets, 2, blk, blk), lambda r: (slab, r, 0, 0, 0, 0)),
        ],
        out_specs=pl.BlockSpec((1, 2 * blk, offsets * blk), lambda r: (r, 0, 0)),
        out_shape=jax.ShapeDtypeStruct((rows, 2 * blk, offsets * blk), jnp.bfloat16),
        compiler_params=pltpu.CompilerParams(vmem_limit_bytes=VMEM_BYTES),
    )(scalars, pattern, tiles)


def step_kernel(kind, reach, pieces, scalars, *refs):
    window, weights, rest = refs[:reach], refs[reach : reach + pieces], refs[reach + pieces : -2]
    taken, held = refs[-2:]
    rows, _, width, blk = window[0].shape
    per_group = weights[0].shape[2] // blk
    skip = -(-REACH // rows) * rows - REACH
    for place in range(OFF + rows - 1):
        taken[place] = window[(place + skip) // rows][(place + skip) % rows].reshape(2 * width, blk)
    starts = [scalars[2 + piece] * per_group for piece in range(pieces)]
    for row in range(rows):
        total = None
        for piece in range(pieces):
            left = jnp.concatenate([taken[starts[piece] + (row + offset)] for offset in range(per_group)], axis=1)
            part = lax.dot_general(
                left, weights[piece][row], (((1,), (1,)), ((), ())), preferred_element_type=jnp.float32
            )
            total = part if total is None else total + part
        product = (total[:width, :blk] - total[width:, blk:], total[:width, blk:] + total[width:, :blk])
        for part in range(2):
            extra = list(rest)
            value = product[part]
            if "add" in kind:
                value = extra.pop(0)[row, part] + coupling * value
            following = value
            if "source" in kind:
                following = extra.pop(0)[row, part].astype(jnp.float32) + coupling * value
            if "merge" in kind:
                value = jnp.where(scalars[0] == kind["merge"], value, extra.pop(0)[row, part])
            if "pieces" in kind:
                held[row, part] = value
                del extra[: kind["pieces"]]
            else:
                extra.pop(0)[row, part] = value
            if "last" not in kind:
                extra.pop(0)[row, part] = following.astype(jnp.bfloat16)
    if "pieces" in kind:
        each = rows // kind["pieces"]
        for by in range(kind["pieces"]):
            goal = lax.rem(scalars[1] + by, kind["pieces"]) * each
            for row in range(each):
                rest[kind["inputs"] + by][row] = held[goal + row]


def applied(kind, scalars, window, weights, extra):
    own = window[0].shape
    rows, height, depth = weights[0].shape
    if "pieces" in kind:
        count = kind["pieces"]
        out_shape = [jax.ShapeDtypeStruct((own[0] // count,) + own[1:], jnp.float32)] * count
    else:
        out_shape = [jax.ShapeDtypeStruct(own, jnp.float32)]
    if "last" not in kind:
        out_shape.append(jax.ShapeDtypeStruct(own, jnp.bfloat16))
    return pl.pallas_call(
        functools.partial(step_kernel, kind | {"inputs": len(extra)}, len(window), len(weights)),
        in_specs=[SCALARS] + [WHOLE] * (len(window) + len(weights) + len(extra)),
        out_specs=[WHOLE] * len(out_shape),
        out_shape=out_shape,
        scratch_shapes=[VMEM((OFF + rows - 1, 2 * own[2], own[3]), jnp.bfloat16), VMEM(own, jnp.float32)],
        compiler_params=pltpu.CompilerParams(vmem_limit_bytes=VMEM_BYTES),
        cost_estimate=pl.CostEstimate(
            flops=2 * own[0] * OFF * 4 * own[2] * own[3] ** 2,
            bytes_accessed=2 * len(weights) * rows * height * depth,
            transcendentals=0,
        ),
    )(scalars, *window, *weights, *extra)


def assembling_kernel(slabs, scalars, *refs):
    pieces, out, held = refs[:-2], refs[-2], refs[-1]
    count = len(pieces) // slabs
    rows = pieces[0].shape[0]
    for slab in range(slabs):
        for by in range(count):
            held[slab, lax.rem(scalars[1] - by + count, count)] = pieces[slab * count + by][...]
    for slab in range(slabs):
        for row in range(rows):
            for part in range(2):
                whole = jnp.concatenate([held[slab, place, row, part] for place in range(count)], axis=0)
                out[slab, row, part] = whole.T


def assembled(scalars, pieces):
    slabs, count = len(pieces), len(pieces[0])
    rows, _, width, blk = pieces[0][0].shape
    return pl.pallas_call(
        functools.partial(assembling_kernel, slabs),
        in_specs=[SCALARS] + [WHOLE] * (slabs * count),
        out_specs=WHOLE,
        out_shape=jax.ShapeDtypeStruct((slabs, rows, 2, blk, width * count), jnp.float32),
        scratch_shapes=[VMEM((slabs, count, rows, 2, width, blk), jnp.float32)],
        compiler_params=pltpu.CompilerParams(vmem_limit_bytes=VMEM_BYTES),
    )(scalars, *[piece for slab in pieces for piece in slab])


def shifted(value, axis, by):
    size = lax.axis_size(axis)
    return lax.ppermute(value, axis, [((i - by) % size, i) for i in range(size)])


def shards(sources, inverse_tiles, pattern, phase_index):
    sections = lax.axis_size("sec")
    section = lax.axis_index("sec")
    slabs, rows, _, blk, columns = sources.shape
    lateral, across, cores = (lax.axis_size(axis) for axis in ("lat", "cx", "core"))
    cx, core = lax.axis_index("cx"), lax.axis_index("core")
    parts = across * cores
    tile_rows = rows * parts
    width = columns // parts
    scalars = jnp.stack(
        [section, cx * cores + core]
        + [
            lax.rem(cx + (across - by_cx), across) * cores + lax.rem(core + (cores - by_core), cores)
            for by_cx in range(across)
            for by_core in range(cores)
        ]
    ).astype(jnp.int32)
    fold_scalars = jnp.stack(
        [
            phase_index[0],
            lax.axis_index("lat") * tile_rows,
            lax.axis_index(("cx", "core")) * inverse_tiles.shape[2],
        ]
    ).astype(jnp.int32)

    below = -(-REACH // tile_rows)
    above = -(-(OFF - 1 - REACH) // tile_rows)

    def windowed(field, by=0):
        if by:
            pairs = [(sec - by, sec) for sec in range(sections) if 0 <= sec - by < sections]
            field = lax.ppermute(field, "sec", pairs)
        return [shifted(field, "lat", -shift) if shift else field for shift in range(-below, above + 1)]

    tiles = []
    folded = [
        folded_tiles(slab, inverse_tiles, pattern, fold_scalars, lateral * tile_rows) for slab in range(slabs)
    ]

    turned = jnp.swapaxes(sources, 3, 4).reshape(slabs, rows, 2, parts, width, blk)
    around = jnp.stack(windowed(turned[0]) + [turned[slab] for slab in range(1, slabs)], 0)
    around = lax.all_to_all(jnp.moveaxis(around, 3, 0), ("cx", "core"), 0, 0, tiled=True)
    around = jnp.swapaxes(around, 0, 1).reshape(-1, tile_rows, 2, width, blk)
    window = [around[place] for place in range(below + above + 1)]
    turned = [None] + [around[below + above + slab] for slab in range(1, slabs)]

    def swapped(near):
        return [shifted(piece, "core", by_core) if by_core else piece for piece in near for by_core in range(cores)]

    def spread(piece):
        return [shifted(piece, "cx", by_cx) if by_cx else piece for by_cx in range(across)]

    near = spread(folded[0])
    window, near[1:], folded[1:] = lax.optimization_barrier((window, near[1:], folded[1:]))
    tiles.append(swapped(near))
    later = [spread(piece) for piece in folded[1:]]

    def delivered(pieces):
        received = []
        for by, piece in enumerate(pieces):
            pairs = [(place, (place + by) % parts) for place in range(parts)]
            received.append(lax.ppermute(piece, ("cx", "core"), pairs) if by else piece)
        return received

    values = []
    for turn in range(sections):
        values.append([])
        for slab in range(slabs):
            kind, extra = {}, []
            if turn > 0 and slab == 0:
                kind["add"] = True
                extra.append(values[0][0])
            if slab < slabs - 1:
                kind["source"] = True
                extra.append(turned[slab + 1])
            value, field = applied(kind, scalars, window, tiles[slab], extra)
            values[turn].append(value)
            if turn == 0 and slab < slabs - 1:
                near = later[slab]
                _, near[1:] = lax.optimization_barrier((field, near[1:]))
                tiles.append(swapped(near))
            last = turn == sections - 1 and slab == slabs - 1
            window = windowed(field, 1 if slab == slabs - 1 and not last else 0)
    results = [None] * slabs
    for turn in range(sections):
        owner = sections - 1 - turn
        for slab in reversed(range(slabs)):
            if turn == 0 and slab == slabs - 1:
                results[slab] = values[owner][slab]
                continue
            kind, extra = {"add": True}, [values[owner][slab]]
            if turn > 0:
                kind["merge"] = owner
                extra.append(results[slab])
            if turn == sections - 1:
                kind["pieces"] = parts
                if slab == 0:
                    kind["last"] = True
            updated = applied(kind, scalars, window, tiles[slab], extra)
            if turn == sections - 1:
                results[slab] = delivered(updated[:parts])
            else:
                results[slab] = updated[0]
            if "last" not in kind:
                window = windowed(updated[-1], -1 if slab == 0 else 0)
    return assembled(scalars, results)


def solution(mesh):
    sections, lateral, col = mesh.devices.shape
    fine = Mesh(mesh.devices.reshape(sections, lateral, col // 2, 2), ("sec", "lat", "cx", "core"))
    placed = (
        P("sec", ("lat", "cx", "core"), None, None, None),
        P("sec", "lat", ("cx", "core"), None, None, None),
        P("sec", "lat", ("cx", "core")),
        P(),
    )
    return jax.shard_map(
        shards,
        mesh=fine,
        in_specs=placed,
        out_specs=P("sec", ("lat", "cx", "core"), None, None, None),
        check_vma=False,
    )
```

```python
import functools
import math

import jax
import jax.numpy as jnp
from jax import lax
from jax.experimental import pallas as pl
from jax.experimental.pallas import tpu as pltpu
from jax.sharding import Mesh, PartitionSpec as P

OFF = 8
PHASES = 16
REACH = OFF // 2
VMEM_BYTES = 12 * 1024 * 1024

coupling = 0.8

VMEM = pltpu.VMEM
SMEM = pltpu.SMEM
WHOLE = pl.BlockSpec(memory_space=VMEM)
SCALARS = pl.BlockSpec(memory_space=SMEM)


def fold_kernel(rows_all, slab, scalars, pattern, tiles, out):
    row = pl.program_id(0)
    offsets = tiles.shape[2]
    blk = tiles.shape[4]
    index = lax.rem(scalars[0], PHASES)
    cos_value = jnp.float32(1.0)
    sin_value = jnp.float32(0.0)
    for step in range(1, PHASES):
        cos_value = jnp.where(index == step, jnp.float32(math.cos(2 * math.pi * step / PHASES)), cos_value)
        sin_value = jnp.where(index == step, jnp.float32(math.sin(2 * math.pi * step / PHASES)), sin_value)
    for offset in range(offsets):
        origin = scalars[1] + row + scalars[2] + offset - REACH
        below = origin < 0
        above = origin >= rows_all
        mask = pattern[slab, row, offset].astype(jnp.float32)
        real_scale = jnp.where(below | above, cos_value, 1.0) * mask
        imag_scale = jnp.where(below, -sin_value, jnp.where(above, sin_value, 0.0)) * mask
        real_part = tiles[0, 0, offset, 0].astype(jnp.float32)
        imag_part = tiles[0, 0, offset, 1].astype(jnp.float32)
        lanes = pl.ds(offset * blk, blk)
        out[0, pl.ds(0, blk), lanes] = (real_part * real_scale - imag_part * imag_scale).astype(jnp.bfloat16)
        out[0, pl.ds(blk, blk), lanes] = (real_part * imag_scale + imag_part * real_scale).astype(jnp.bfloat16)


def folded_tiles(slab, tiles, pattern, scalars, rows_all):
    _, rows, offsets, _, blk, _ = tiles.shape
    return pl.pallas_call(
        functools.partial(fold_kernel, rows_all, slab),
        grid=(rows,),
        in_specs=[
            SCALARS,
            SCALARS,
            pl.BlockSpec((1, 1, offsets, 2, blk, blk), lambda r: (slab, r, 0, 0, 0, 0)),
        ],
        out_specs=pl.BlockSpec((1, 2 * blk, offsets * blk), lambda r: (r, 0, 0)),
        out_shape=jax.ShapeDtypeStruct((rows, 2 * blk, offsets * blk), jnp.bfloat16),
        compiler_params=pltpu.CompilerParams(vmem_limit_bytes=VMEM_BYTES),
    )(scalars, pattern, tiles)


def step_kernel(kind, reach, pieces, scalars, *refs):
    window, weights, rest = refs[:reach], refs[reach : reach + pieces], refs[reach + pieces : -2]
    taken, held = refs[-2:]
    rows, _, width, blk = window[0].shape
    per_group = weights[0].shape[2] // blk
    skip = -(-REACH // rows) * rows - REACH
    for place in range(OFF + rows - 1):
        taken[place] = window[(place + skip) // rows][(place + skip) % rows].reshape(2 * width, blk)
    starts = [scalars[2 + piece] * per_group for piece in range(pieces)]
    for row in range(rows):
        total = None
        for piece in range(pieces):
            left = jnp.concatenate([taken[starts[piece] + (row + offset)] for offset in range(per_group)], axis=1)
            part = lax.dot_general(
                left, weights[piece][row], (((1,), (1,)), ((), ())), preferred_element_type=jnp.float32
            )
            total = part if total is None else total + part
        product = (total[:width, :blk] - total[width:, blk:], total[:width, blk:] + total[width:, :blk])
        for part in range(2):
            extra = list(rest)
            value = product[part]
            if "add" in kind:
                value = extra.pop(0)[row, part] + coupling * value
            following = value
            if "source" in kind:
                following = extra.pop(0)[row, part].astype(jnp.float32) + coupling * value
            if "merge" in kind:
                value = jnp.where(scalars[0] == kind["merge"], value, extra.pop(0)[row, part])
            if "pieces" in kind:
                held[row, part] = value
                del extra[: kind["pieces"]]
            else:
                extra.pop(0)[row, part] = value
            if "last" not in kind:
                extra.pop(0)[row, part] = following.astype(jnp.bfloat16)
    if "pieces" in kind:
        each = rows // kind["pieces"]
        for by in range(kind["pieces"]):
            goal = lax.rem(scalars[1] + by, kind["pieces"]) * each
            for row in range(each):
                rest[kind["inputs"] + by][row] = held[goal + row]


def applied(kind, scalars, window, weights, extra):
    own = window[0].shape
    rows, height, depth = weights[0].shape
    if "pieces" in kind:
        count = kind["pieces"]
        out_shape = [jax.ShapeDtypeStruct((own[0] // count,) + own[1:], jnp.float32)] * count
    else:
        out_shape = [jax.ShapeDtypeStruct(own, jnp.float32)]
    if "last" not in kind:
        out_shape.append(jax.ShapeDtypeStruct(own, jnp.bfloat16))
    return pl.pallas_call(
        functools.partial(step_kernel, kind | {"inputs": len(extra)}, len(window), len(weights)),
        in_specs=[SCALARS] + [WHOLE] * (len(window) + len(weights) + len(extra)),
        out_specs=[WHOLE] * len(out_shape),
        out_shape=out_shape,
        scratch_shapes=[VMEM((OFF + rows - 1, 2 * own[2], own[3]), jnp.bfloat16), VMEM(own, jnp.float32)],
        compiler_params=pltpu.CompilerParams(vmem_limit_bytes=VMEM_BYTES),
        cost_estimate=pl.CostEstimate(
            flops=2 * own[0] * OFF * 4 * own[2] * own[3] ** 2,
            bytes_accessed=2 * len(weights) * rows * height * depth,
            transcendentals=0,
        ),
    )(scalars, *window, *weights, *extra)


def assembling_kernel(slabs, scalars, *refs):
    pieces, out, held = refs[:-2], refs[-2], refs[-1]
    count = len(pieces) // slabs
    rows = pieces[0].shape[0]
    for slab in range(slabs):
        for by in range(count):
            held[slab, lax.rem(scalars[1] - by + count, count)] = pieces[slab * count + by][...]
    for slab in range(slabs):
        for row in range(rows):
            for part in range(2):
                whole = jnp.concatenate([held[slab, place, row, part] for place in range(count)], axis=0)
                out[slab, row, part] = whole.T


def assembled(scalars, pieces):
    slabs, count = len(pieces), len(pieces[0])
    rows, _, width, blk = pieces[0][0].shape
    return pl.pallas_call(
        functools.partial(assembling_kernel, slabs),
        in_specs=[SCALARS] + [WHOLE] * (slabs * count),
        out_specs=WHOLE,
        out_shape=jax.ShapeDtypeStruct((slabs, rows, 2, blk, width * count), jnp.float32),
        scratch_shapes=[VMEM((slabs, count, rows, 2, width, blk), jnp.float32)],
        compiler_params=pltpu.CompilerParams(vmem_limit_bytes=VMEM_BYTES),
    )(scalars, *[piece for slab in pieces for piece in slab])


def picking_kernel(across, cores, slab, scalars, *refs):
    pieces, out = refs[:-1], refs[-1]
    rows = pieces[0].shape[1]
    for place, piece in enumerate(pieces):
        origin = scalars[2 + place] * rows
        for row in range(rows):
            for part in range(2):
                out[origin + row, part] = piece[slab, row, part, scalars[1]]


def picked(scalars, across, cores, slab, pieces):
    _, rows, _, parts, width, blk = pieces[0].shape
    return pl.pallas_call(
        functools.partial(picking_kernel, across, cores, slab),
        in_specs=[SCALARS] + [WHOLE] * len(pieces),
        out_specs=WHOLE,
        out_shape=jax.ShapeDtypeStruct((rows * parts, 2, width, blk), jnp.bfloat16),
        compiler_params=pltpu.CompilerParams(vmem_limit_bytes=VMEM_BYTES),
    )(scalars, *pieces)


def shifted(value, axis, by):
    size = lax.axis_size(axis)
    return lax.ppermute(value, axis, [((i - by) % size, i) for i in range(size)])


def shards(sources, inverse_tiles, pattern, phase_index):
    sections = lax.axis_size("sec")
    section = lax.axis_index("sec")
    slabs, rows, _, blk, columns = sources.shape
    lateral, across, cores = (lax.axis_size(axis) for axis in ("lat", "cx", "core"))
    cx, core = lax.axis_index("cx"), lax.axis_index("core")
    parts = across * cores
    tile_rows = rows * parts
    width = columns // parts
    scalars = jnp.stack(
        [section, cx * cores + core]
        + [
            lax.rem(cx + (across - by_cx), across) * cores + lax.rem(core + (cores - by_core), cores)
            for by_cx in range(across)
            for by_core in range(cores)
        ]
    ).astype(jnp.int32)
    fold_scalars = jnp.stack(
        [
            phase_index[0],
            lax.axis_index("lat") * tile_rows,
            lax.axis_index(("cx", "core")) * inverse_tiles.shape[2],
        ]
    ).astype(jnp.int32)

    below = -(-REACH // tile_rows)
    above = -(-(OFF - 1 - REACH) // tile_rows)

    def windowed(field, by=0):
        if by:
            pairs = [(sec - by, sec) for sec in range(sections) if 0 <= sec - by < sections]
            field = lax.ppermute(field, "sec", pairs)
        return [shifted(field, "lat", -shift) if shift else field for shift in range(-below, above + 1)]

    tiles = []
    folded = [
        folded_tiles(slab, inverse_tiles, pattern, fold_scalars, lateral * tile_rows) for slab in range(slabs)
    ]

    def swapped(near):
        return [shifted(piece, "core", by_core) if by_core else piece for piece in near for by_core in range(cores)]

    def spread(piece):
        return [shifted(piece, "cx", by_cx) if by_cx else piece for by_cx in range(across)]

    around = spread(jnp.swapaxes(sources, 3, 4).reshape(slabs, rows, 2, parts, width, blk))
    around[1:], folded = lax.optimization_barrier((around[1:], folded))
    around = swapped(around)
    turned = [picked(scalars, across, cores, slab, around) for slab in range(slabs)]
    window = windowed(turned[0])

    spreads = [spread(piece) for piece in folded]

    def finished(slab, ready):
        near = spreads[slab]
        _, near[1:] = lax.optimization_barrier((ready, near[1:]))
        tiles.append(swapped(near))

    finished(0, window)

    def delivered(pieces):
        received = []
        for by, piece in enumerate(pieces):
            pairs = [(place, (place + by) % parts) for place in range(parts)]
            received.append(lax.ppermute(piece, ("cx", "core"), pairs) if by else piece)
        return received

    values = []
    for turn in range(sections):
        values.append([])
        for slab in range(slabs):
            kind, extra = {}, []
            if turn > 0 and slab == 0:
                kind["add"] = True
                extra.append(values[0][0])
            if slab < slabs - 1:
                kind["source"] = True
                extra.append(turned[slab + 1])
            value, field = applied(kind, scalars, window, tiles[slab], extra)
            values[turn].append(value)
            last = turn == sections - 1 and slab == slabs - 1
            window = windowed(field, 1 if slab == slabs - 1 and not last else 0)
            if turn == 0 and slab < slabs - 1:
                finished(slab + 1, window)
    results = [None] * slabs
    for turn in range(sections):
        owner = sections - 1 - turn
        for slab in reversed(range(slabs)):
            if turn == 0 and slab == slabs - 1:
                results[slab] = values[owner][slab]
                continue
            kind, extra = {"add": True}, [values[owner][slab]]
            if turn > 0:
                kind["merge"] = owner
                extra.append(results[slab])
            if turn == sections - 1:
                kind["pieces"] = parts
                if slab == 0:
                    kind["last"] = True
            updated = applied(kind, scalars, window, tiles[slab], extra)
            if turn == sections - 1:
                results[slab] = delivered(updated[:parts])
            else:
                results[slab] = updated[0]
            if "last" not in kind:
                window = windowed(updated[-1], -1 if slab == 0 else 0)
    return assembled(scalars, results)


def solution(mesh):
    sections, lateral, col = mesh.devices.shape
    fine = Mesh(mesh.devices.reshape(sections, lateral, col // 2, 2), ("sec", "lat", "cx", "core"))
    placed = (
        P("sec", ("lat", "cx", "core"), None, None, None),
        P("sec", "lat", ("cx", "core"), None, None, None),
        P("sec", "lat", ("cx", "core")),
        P(),
    )
    return jax.shard_map(
        shards,
        mesh=fine,
        in_specs=placed,
        out_specs=P("sec", ("lat", "cx", "core"), None, None, None),
        check_vma=False,
    )
```

```python
import functools
import math

import jax
import jax.numpy as jnp
from jax import lax
from jax.experimental import pallas as pl
from jax.experimental.pallas import tpu as pltpu
from jax.sharding import Mesh, PartitionSpec as P

OFF = 8
PHASES = 16
REACH = OFF // 2
VMEM_BYTES = 12 * 1024 * 1024

coupling = 0.8

VMEM = pltpu.VMEM
SMEM = pltpu.SMEM
WHOLE = pl.BlockSpec(memory_space=VMEM)
SCALARS = pl.BlockSpec(memory_space=SMEM)


def fold_kernel(rows_all, slab, scalars, pattern, tiles, out):
    row = pl.program_id(0)
    offsets = tiles.shape[2]
    blk = tiles.shape[4]
    index = lax.rem(scalars[0], PHASES)
    cos_value = jnp.float32(1.0)
    sin_value = jnp.float32(0.0)
    for step in range(1, PHASES):
        cos_value = jnp.where(index == step, jnp.float32(math.cos(2 * math.pi * step / PHASES)), cos_value)
        sin_value = jnp.where(index == step, jnp.float32(math.sin(2 * math.pi * step / PHASES)), sin_value)
    for offset in range(offsets):
        origin = scalars[1] + row + scalars[2] + offset - REACH
        below = origin < 0
        above = origin >= rows_all
        mask = pattern[slab, row, offset].astype(jnp.float32)
        real_scale = jnp.where(below | above, cos_value, 1.0) * mask
        imag_scale = jnp.where(below, -sin_value, jnp.where(above, sin_value, 0.0)) * mask
        real_part = tiles[0, 0, offset, 0].astype(jnp.float32)
        imag_part = tiles[0, 0, offset, 1].astype(jnp.float32)
        lanes = pl.ds(offset * blk, blk)
        out[0, pl.ds(0, blk), lanes] = (real_part * real_scale - imag_part * imag_scale).astype(jnp.bfloat16)
        out[0, pl.ds(blk, blk), lanes] = (real_part * imag_scale + imag_part * real_scale).astype(jnp.bfloat16)


def folded_tiles(slab, tiles, pattern, scalars, rows_all):
    _, rows, offsets, _, blk, _ = tiles.shape
    return pl.pallas_call(
        functools.partial(fold_kernel, rows_all, slab),
        grid=(rows,),
        in_specs=[
            SCALARS,
            SCALARS,
            pl.BlockSpec((1, 1, offsets, 2, blk, blk), lambda r: (slab, r, 0, 0, 0, 0)),
        ],
        out_specs=pl.BlockSpec((1, 2 * blk, offsets * blk), lambda r: (r, 0, 0)),
        out_shape=jax.ShapeDtypeStruct((rows, 2 * blk, offsets * blk), jnp.bfloat16),
        compiler_params=pltpu.CompilerParams(vmem_limit_bytes=VMEM_BYTES),
    )(scalars, pattern, tiles)


def step_kernel(kind, reach, pieces, scalars, *refs):
    window, weights, rest = refs[:reach], refs[reach : reach + pieces], refs[reach + pieces : -2]
    taken, held = refs[-2:]
    rows, _, width, blk = window[0].shape
    per_group = weights[0].shape[2] // blk
    skip = -(-REACH // rows) * rows - REACH
    for place in range(OFF + rows - 1):
        taken[place] = window[(place + skip) // rows][(place + skip) % rows].reshape(2 * width, blk)
    starts = [scalars[2 + piece] * per_group for piece in range(pieces)]
    for row in range(rows):
        total = None
        for piece in range(pieces):
            left = jnp.concatenate([taken[starts[piece] + (row + offset)] for offset in range(per_group)], axis=1)
            part = lax.dot_general(
                left, weights[piece][row], (((1,), (1,)), ((), ())), preferred_element_type=jnp.float32
            )
            total = part if total is None else total + part
        product = (total[:width, :blk] - total[width:, blk:], total[:width, blk:] + total[width:, :blk])
        for part in range(2):
            extra = list(rest)
            value = product[part]
            if "add" in kind:
                value = extra.pop(0)[row, part] + coupling * value
            following = value
            if "source" in kind:
                following = extra.pop(0)[row, part].astype(jnp.float32) + coupling * value
            if "merge" in kind:
                value = jnp.where(scalars[0] == kind["merge"], value, extra.pop(0)[row, part])
            if "pieces" in kind:
                held[row, part] = value
                del extra[: kind["pieces"]]
            else:
                extra.pop(0)[row, part] = value
            if "last" not in kind:
                field, edge = extra
                field[row, part] = following.astype(jnp.bfloat16)
                if row < edge.shape[0]:
                    edge[row, part] = following.astype(jnp.bfloat16)
    if "pieces" in kind:
        each = rows // kind["pieces"]
        for by in range(kind["pieces"]):
            goal = lax.rem(scalars[1] + by, kind["pieces"]) * each
            for row in range(each):
                rest[kind["inputs"] + by][row] = held[goal + row]


def applied(kind, scalars, window, weights, extra):
    own = window[0].shape
    rows, height, depth = weights[0].shape
    if "pieces" in kind:
        count = kind["pieces"]
        out_shape = [jax.ShapeDtypeStruct((own[0] // count,) + own[1:], jnp.float32)] * count
    else:
        out_shape = [jax.ShapeDtypeStruct(own, jnp.float32)]
    if "last" not in kind:
        out_shape.append(jax.ShapeDtypeStruct(own, jnp.bfloat16))
        out_shape.append(jax.ShapeDtypeStruct(window[-1].shape, jnp.bfloat16))
    return pl.pallas_call(
        functools.partial(step_kernel, kind | {"inputs": len(extra)}, len(window), len(weights)),
        in_specs=[SCALARS] + [WHOLE] * (len(window) + len(weights) + len(extra)),
        out_specs=[WHOLE] * len(out_shape),
        out_shape=out_shape,
        scratch_shapes=[VMEM((OFF + rows - 1, 2 * own[2], own[3]), jnp.bfloat16), VMEM(own, jnp.float32)],
        compiler_params=pltpu.CompilerParams(vmem_limit_bytes=VMEM_BYTES),
        cost_estimate=pl.CostEstimate(
            flops=2 * own[0] * OFF * 4 * own[2] * own[3] ** 2,
            bytes_accessed=2 * len(weights) * rows * height * depth,
            transcendentals=0,
        ),
    )(scalars, *window, *weights, *extra)


def assembling_kernel(slabs, scalars, *refs):
    pieces, out, held = refs[:-2], refs[-2], refs[-1]
    count = len(pieces) // slabs
    rows = pieces[0].shape[0]
    for slab in range(slabs):
        for by in range(count):
            held[slab, lax.rem(scalars[1] - by + count, count)] = pieces[slab * count + by][...]
    for slab in range(slabs):
        for row in range(rows):
            for part in range(2):
                whole = jnp.concatenate([held[slab, place, row, part] for place in range(count)], axis=0)
                out[slab, row, part] = whole.T


def assembled(scalars, pieces):
    slabs, count = len(pieces), len(pieces[0])
    rows, _, width, blk = pieces[0][0].shape
    return pl.pallas_call(
        functools.partial(assembling_kernel, slabs),
        in_specs=[SCALARS] + [WHOLE] * (slabs * count),
        out_specs=WHOLE,
        out_shape=jax.ShapeDtypeStruct((slabs, rows, 2, blk, width * count), jnp.float32),
        scratch_shapes=[VMEM((slabs, count, rows, 2, width, blk), jnp.float32)],
        compiler_params=pltpu.CompilerParams(vmem_limit_bytes=VMEM_BYTES),
    )(scalars, *[piece for slab in pieces for piece in slab])


def picking_kernel(across, cores, slab, scalars, *refs):
    pieces, out = refs[:-1], refs[-1]
    rows = pieces[0].shape[1]
    for place, piece in enumerate(pieces):
        origin = scalars[2 + place] * rows
        for row in range(rows):
            for part in range(2):
                out[origin + row, part] = piece[slab, row, part, scalars[1]]


def picked(scalars, across, cores, slab, pieces):
    _, rows, _, parts, width, blk = pieces[0].shape
    return pl.pallas_call(
        functools.partial(picking_kernel, across, cores, slab),
        in_specs=[SCALARS] + [WHOLE] * len(pieces),
        out_specs=WHOLE,
        out_shape=jax.ShapeDtypeStruct((rows * parts, 2, width, blk), jnp.bfloat16),
        compiler_params=pltpu.CompilerParams(vmem_limit_bytes=VMEM_BYTES),
    )(scalars, *pieces)


def shifted(value, axis, by):
    size = lax.axis_size(axis)
    return lax.ppermute(value, axis, [((i - by) % size, i) for i in range(size)])


def shards(sources, inverse_tiles, pattern, phase_index):
    sections = lax.axis_size("sec")
    section = lax.axis_index("sec")
    slabs, rows, _, blk, columns = sources.shape
    lateral, across, cores = (lax.axis_size(axis) for axis in ("lat", "cx", "core"))
    cx, core = lax.axis_index("cx"), lax.axis_index("core")
    parts = across * cores
    tile_rows = rows * parts
    width = columns // parts
    scalars = jnp.stack(
        [section, cx * cores + core]
        + [
            lax.rem(cx + (across - by_cx), across) * cores + lax.rem(core + (cores - by_core), cores)
            for by_cx in range(across)
            for by_core in range(cores)
        ]
    ).astype(jnp.int32)
    fold_scalars = jnp.stack(
        [
            phase_index[0],
            lax.axis_index("lat") * tile_rows,
            lax.axis_index(("cx", "core")) * inverse_tiles.shape[2],
        ]
    ).astype(jnp.int32)

    below = -(-REACH // tile_rows)
    above = -(-(OFF - 1 - REACH) // tile_rows)
    edge_rows = OFF - 1 - REACH - (above - 1) * tile_rows

    def windowed(field, by=0):
        window = []
        for shift in range(-below, above + 1):
            pairs = []
            for sec in range(sections):
                if 0 <= sec - by < sections:
                    pairs += [
                        ((sec - by) * lateral + (lat + shift) % lateral, sec * lateral + lat) for lat in range(lateral)
                    ]
            sent = field[1] if shift == above else field[0]
            window.append(lax.ppermute(sent, ("sec", "lat"), pairs) if by or shift else sent)
        return window

    tiles = []
    folded = [
        folded_tiles(slab, inverse_tiles, pattern, fold_scalars, lateral * tile_rows) for slab in range(slabs)
    ]

    def swapped(near):
        return [shifted(piece, "core", by_core) if by_core else piece for piece in near for by_core in range(cores)]

    def spread(piece):
        return [shifted(piece, "cx", by_cx) if by_cx else piece for by_cx in range(across)]

    around = spread(jnp.swapaxes(sources, 3, 4).reshape(slabs, rows, 2, parts, width, blk))
    around[1:], folded[0] = lax.optimization_barrier((around[1:], folded[0]))
    around = swapped(around)
    turned = [picked(scalars, across, cores, slab, around) for slab in range(slabs)]
    window = windowed((turned[0], turned[0][:edge_rows]))

    spreads = [spread(piece) for piece in folded]

    def finished(slab, ready):
        near = spreads[slab]
        _, near[1:] = lax.optimization_barrier((ready, near[1:]))
        tiles.append(swapped(near))

    finished(0, window)

    def delivered(pieces):
        received = []
        for by, piece in enumerate(pieces):
            pairs = [(place, (place + by) % parts) for place in range(parts)]
            received.append(lax.ppermute(piece, ("cx", "core"), pairs) if by else piece)
        return received

    values = []
    for turn in range(sections):
        values.append([])
        for slab in range(slabs):
            kind, extra = {}, []
            if turn > 0 and slab == 0:
                kind["add"] = True
                extra.append(values[0][0])
            if slab < slabs - 1:
                kind["source"] = True
                extra.append(turned[slab + 1])
            value, *field = applied(kind, scalars, window, tiles[slab], extra)
            values[turn].append(value)
            last = turn == sections - 1 and slab == slabs - 1
            window = windowed(field, 1 if slab == slabs - 1 and not last else 0)
            if turn == 0 and slab < slabs - 1:
                finished(slab + 1, window)
    results = [None] * slabs
    for turn in range(sections):
        owner = sections - 1 - turn
        for slab in reversed(range(slabs)):
            if turn == 0 and slab == slabs - 1:
                results[slab] = values[owner][slab]
                continue
            kind, extra = {"add": True}, [values[owner][slab]]
            if turn > 0:
                kind["merge"] = owner
                extra.append(results[slab])
            if turn == sections - 1:
                kind["pieces"] = parts
                if slab == 0:
                    kind["last"] = True
            updated = applied(kind, scalars, window, tiles[slab], extra)
            if turn == sections - 1:
                results[slab] = delivered(updated[:parts])
            else:
                results[slab] = updated[0]
            if "last" not in kind:
                window = windowed(updated[-2:], -1 if slab == 0 else 0)
    return assembled(scalars, results)


def solution(mesh):
    sections, lateral, col = mesh.devices.shape
    fine = Mesh(mesh.devices.reshape(sections, lateral, col // 2, 2), ("sec", "lat", "cx", "core"))
    placed = (
        P("sec", ("lat", "cx", "core"), None, None, None),
        P("sec", "lat", ("cx", "core"), None, None, None),
        P("sec", "lat", ("cx", "core")),
        P(),
    )
    return jax.shard_map(
        shards,
        mesh=fine,
        in_specs=placed,
        out_specs=P("sec", ("lat", "cx", "core"), None, None, None),
        check_vma=False,
    )
```

```python
import functools
import math

import jax
import jax.numpy as jnp
from jax import lax
from jax.experimental import pallas as pl
from jax.experimental.pallas import tpu as pltpu
from jax.sharding import Mesh, PartitionSpec as P

OFF = 8
PHASES = 16
REACH = OFF // 2
VMEM_BYTES = 12 * 1024 * 1024

coupling = 0.8

VMEM = pltpu.VMEM
SMEM = pltpu.SMEM
WHOLE = pl.BlockSpec(memory_space=VMEM)
SCALARS = pl.BlockSpec(memory_space=SMEM)


def fold_kernel(rows_all, slab, scalars, pattern, tiles, out):
    row = pl.program_id(0)
    offsets = tiles.shape[2]
    blk = tiles.shape[4]
    index = lax.rem(scalars[0], PHASES)
    cos_value = jnp.float32(1.0)
    sin_value = jnp.float32(0.0)
    for step in range(1, PHASES):
        cos_value = jnp.where(index == step, jnp.float32(math.cos(2 * math.pi * step / PHASES)), cos_value)
        sin_value = jnp.where(index == step, jnp.float32(math.sin(2 * math.pi * step / PHASES)), sin_value)
    for offset in range(offsets):
        origin = scalars[1] + row + scalars[2] + offset - REACH
        below = origin < 0
        above = origin >= rows_all
        mask = pattern[slab, row, offset].astype(jnp.float32)
        real_scale = jnp.where(below | above, cos_value, 1.0) * mask
        imag_scale = jnp.where(below, -sin_value, jnp.where(above, sin_value, 0.0)) * mask
        real_part = tiles[0, 0, offset, 0].astype(jnp.float32)
        imag_part = tiles[0, 0, offset, 1].astype(jnp.float32)
        lanes = pl.ds(offset * blk, blk)
        out[0, pl.ds(0, blk), lanes] = (real_part * real_scale - imag_part * imag_scale).astype(jnp.bfloat16)
        out[0, pl.ds(blk, blk), lanes] = (real_part * imag_scale + imag_part * real_scale).astype(jnp.bfloat16)


def folded_tiles(slab, tiles, pattern, scalars, rows_all):
    _, rows, offsets, _, blk, _ = tiles.shape
    return pl.pallas_call(
        functools.partial(fold_kernel, rows_all, slab),
        grid=(rows,),
        in_specs=[
            SCALARS,
            SCALARS,
            pl.BlockSpec((1, 1, offsets, 2, blk, blk), lambda r: (slab, r, 0, 0, 0, 0)),
        ],
        out_specs=pl.BlockSpec((1, 2 * blk, offsets * blk), lambda r: (r, 0, 0)),
        out_shape=jax.ShapeDtypeStruct((rows, 2 * blk, offsets * blk), jnp.bfloat16),
        compiler_params=pltpu.CompilerParams(vmem_limit_bytes=VMEM_BYTES),
    )(scalars, pattern, tiles)


def step_kernel(kind, reach, pieces, scalars, *refs):
    window, weights, rest = refs[:reach], refs[reach : reach + pieces], refs[reach + pieces : -2]
    taken, held = refs[-2:]
    own, befores, afters = window[0], window[1 : 1 + reach // 2], window[-(reach // 2) :]
    rows, _, width, blk = own.shape
    per_group = weights[0].shape[2] // blk
    skip = -(-REACH // rows) * rows - REACH
    for place in range(OFF + rows - 1):
        side, row = divmod(place + skip, rows)
        options = (befores, (own,), afters)[side]
        value = options[0][row]
        if len(options) > 1:
            value = jnp.where(scalars[2 + side // 2] == 1, options[1][row], value)
        taken[place] = value.reshape(2 * width, blk)
    starts = [scalars[4 + piece] * per_group for piece in range(pieces)]
    for row in range(rows):
        total = None
        for piece in range(pieces):
            left = jnp.concatenate([taken[starts[piece] + (row + offset)] for offset in range(per_group)], axis=1)
            part = lax.dot_general(
                left, weights[piece][row], (((1,), (1,)), ((), ())), preferred_element_type=jnp.float32
            )
            total = part if total is None else total + part
        product = (total[:width, :blk] - total[width:, blk:], total[:width, blk:] + total[width:, :blk])
        for part in range(2):
            extra = list(rest)
            value = product[part]
            if "add" in kind:
                value = extra.pop(0)[row, part] + coupling * value
            following = value
            if "source" in kind:
                following = extra.pop(0)[row, part].astype(jnp.float32) + coupling * value
            if "merge" in kind:
                value = jnp.where(scalars[0] == kind["merge"], value, extra.pop(0)[row, part])
            if "pieces" in kind:
                held[row, part] = value
                del extra[: kind["pieces"]]
            else:
                extra.pop(0)[row, part] = value
            if "last" not in kind:
                field, edge = extra
                field[row, part] = following.astype(jnp.bfloat16)
                if row < edge.shape[0]:
                    edge[row, part] = following.astype(jnp.bfloat16)
    if "pieces" in kind:
        each = rows // kind["pieces"]
        for by in range(kind["pieces"]):
            goal = lax.rem(scalars[1] + by, kind["pieces"]) * each
            for row in range(each):
                rest[kind["inputs"] + by][row] = held[goal + row]


def applied(kind, scalars, window, weights, extra, edge_rows):
    own = window[0].shape
    rows, height, depth = weights[0].shape
    if "pieces" in kind:
        count = kind["pieces"]
        out_shape = [jax.ShapeDtypeStruct((own[0] // count,) + own[1:], jnp.float32)] * count
    else:
        out_shape = [jax.ShapeDtypeStruct(own, jnp.float32)]
    if "last" not in kind:
        out_shape.append(jax.ShapeDtypeStruct(own, jnp.bfloat16))
        out_shape.append(jax.ShapeDtypeStruct((edge_rows,) + own[1:], jnp.bfloat16))
    return pl.pallas_call(
        functools.partial(step_kernel, kind | {"inputs": len(extra)}, len(window), len(weights)),
        in_specs=[SCALARS] + [WHOLE] * (len(window) + len(weights) + len(extra)),
        out_specs=[WHOLE] * len(out_shape),
        out_shape=out_shape,
        scratch_shapes=[VMEM((OFF + rows - 1, 2 * own[2], own[3]), jnp.bfloat16), VMEM(own, jnp.float32)],
        compiler_params=pltpu.CompilerParams(vmem_limit_bytes=VMEM_BYTES),
        cost_estimate=pl.CostEstimate(
            flops=2 * own[0] * OFF * 4 * own[2] * own[3] ** 2,
            bytes_accessed=2 * len(weights) * rows * height * depth,
            transcendentals=0,
        ),
    )(scalars, *window, *weights, *extra)


def assembling_kernel(slabs, scalars, *refs):
    pieces, out, held = refs[:-2], refs[-2], refs[-1]
    count = len(pieces) // slabs
    rows = pieces[0].shape[0]
    for slab in range(slabs):
        for by in range(count):
            held[slab, lax.rem(scalars[1] - by + count, count)] = pieces[slab * count + by][...]
    for slab in range(slabs):
        for row in range(rows):
            for part in range(2):
                whole = jnp.concatenate([held[slab, place, row, part] for place in range(count)], axis=0)
                out[slab, row, part] = whole.T


def assembled(scalars, pieces):
    slabs, count = len(pieces), len(pieces[0])
    rows, _, width, blk = pieces[0][0].shape
    return pl.pallas_call(
        functools.partial(assembling_kernel, slabs),
        in_specs=[SCALARS] + [WHOLE] * (slabs * count),
        out_specs=WHOLE,
        out_shape=jax.ShapeDtypeStruct((slabs, rows, 2, blk, width * count), jnp.float32),
        scratch_shapes=[VMEM((slabs, count, rows, 2, width, blk), jnp.float32)],
        compiler_params=pltpu.CompilerParams(vmem_limit_bytes=VMEM_BYTES),
    )(scalars, *[piece for slab in pieces for piece in slab])


def picking_kernel(across, cores, slab, scalars, *refs):
    pieces, out = refs[:-1], refs[-1]
    rows = pieces[0].shape[1]
    for place, piece in enumerate(pieces):
        origin = scalars[4 + place] * rows
        for row in range(rows):
            for part in range(2):
                out[origin + row, part] = piece[slab, row, part, scalars[1]]


def picked(scalars, across, cores, slab, pieces):
    _, rows, _, parts, width, blk = pieces[0].shape
    return pl.pallas_call(
        functools.partial(picking_kernel, across, cores, slab),
        in_specs=[SCALARS] + [WHOLE] * len(pieces),
        out_specs=WHOLE,
        out_shape=jax.ShapeDtypeStruct((rows * parts, 2, width, blk), jnp.bfloat16),
        compiler_params=pltpu.CompilerParams(vmem_limit_bytes=VMEM_BYTES),
    )(scalars, *pieces)


def shifted(value, axis, by):
    size = lax.axis_size(axis)
    return lax.ppermute(value, axis, [((i - by) % size, i) for i in range(size)])


def shards(sources, inverse_tiles, pattern, phase_index):
    sections = lax.axis_size("sec")
    section = lax.axis_index("sec")
    slabs, rows, _, blk, columns = sources.shape
    lateral, across, cores = (lax.axis_size(axis) for axis in ("lat", "cx", "core"))
    cx, core, lat = lax.axis_index("cx"), lax.axis_index("core"), lax.axis_index("lat")
    parts = across * cores
    tile_rows = rows * parts
    width = columns // parts
    scalars = jnp.stack(
        [section, cx * cores + core, lat == 0, lat == lateral - 1]
        + [
            lax.rem(cx + (across - by_cx), across) * cores + lax.rem(core + (cores - by_core), cores)
            for by_cx in range(across)
            for by_core in range(cores)
        ]
    ).astype(jnp.int32)
    fold_scalars = jnp.stack(
        [
            phase_index[0],
            lax.axis_index("lat") * tile_rows,
            lax.axis_index(("cx", "core")) * inverse_tiles.shape[2],
        ]
    ).astype(jnp.int32)

    assert tile_rows >= REACH
    edge_rows = OFF - 1 - REACH

    def windowed(field, by=0):
        whole, edge = field
        own = [(place, place) for place in range(lateral)]
        up = [(place, place + 1) for place in range(lateral - 1)]
        down = [(place + 1, place) for place in range(lateral - 1)]
        round_up, round_down = [(lateral - 1, 0)], [(0, lateral - 1)]

        def sent(value, moves):
            pairs = [
                ((sec - by) * lateral + origin, sec * lateral + goal)
                for sec in range(sections)
                if 0 <= sec - by < sections
                for origin, goal in moves
            ]
            return lax.ppermute(value, ("sec", "lat"), pairs)

        if by:
            return [sent(whole, own), sent(whole, up + round_up), sent(edge, down + round_down)]
        wrapped = sent(whole, round_up + round_down)
        return [whole, sent(whole, up), wrapped, sent(edge, down), wrapped]

    tiles = []
    folded = [
        folded_tiles(slab, inverse_tiles, pattern, fold_scalars, lateral * tile_rows) for slab in range(slabs)
    ]

    def swapped(near):
        return [shifted(piece, "core", by_core) if by_core else piece for piece in near for by_core in range(cores)]

    def spread(piece):
        return [shifted(piece, "cx", by_cx) if by_cx else piece for by_cx in range(across)]

    around = spread(jnp.swapaxes(sources, 3, 4).reshape(slabs, rows, 2, parts, width, blk))
    around[1:], folded[0] = lax.optimization_barrier((around[1:], folded[0]))
    around = swapped(around)
    turned = [picked(scalars, across, cores, slab, around) for slab in range(slabs)]
    turned[0], folded[1:] = lax.optimization_barrier((turned[0], folded[1:]))
    window = windowed((turned[0], turned[0][:edge_rows]))

    spreads = [spread(piece) for piece in folded]

    def finished(slab, ready):
        near = spreads[slab]
        _, near[1:] = lax.optimization_barrier((ready, near[1:]))
        tiles.append(swapped(near))

    finished(0, window)

    def delivered(pieces):
        received = []
        for by, piece in enumerate(pieces):
            pairs = [(place, (place + by) % parts) for place in range(parts)]
            received.append(lax.ppermute(piece, ("cx", "core"), pairs) if by else piece)
        return received

    values = []
    for turn in range(sections):
        values.append([])
        for slab in range(slabs):
            kind, extra = {}, []
            if turn > 0 and slab == 0:
                kind["add"] = True
                extra.append(values[0][0])
            if slab < slabs - 1:
                kind["source"] = True
                extra.append(turned[slab + 1])
            value, *field = applied(kind, scalars, window, tiles[slab], extra, edge_rows)
            values[turn].append(value)
            last = turn == sections - 1 and slab == slabs - 1
            window = windowed(field, 1 if slab == slabs - 1 and not last else 0)
            if turn == 0 and slab < slabs - 1:
                finished(slab + 1, window)
    results = [None] * slabs
    for turn in range(sections):
        owner = sections - 1 - turn
        for slab in reversed(range(slabs)):
            if turn == 0 and slab == slabs - 1:
                results[slab] = values[owner][slab]
                continue
            kind, extra = {"add": True}, [values[owner][slab]]
            if turn > 0:
                kind["merge"] = owner
                extra.append(results[slab])
            if turn == sections - 1:
                kind["pieces"] = parts
                if slab == 0:
                    kind["last"] = True
            updated = applied(kind, scalars, window, tiles[slab], extra, edge_rows)
            if turn == sections - 1:
                results[slab] = delivered(updated[:parts])
            else:
                results[slab] = updated[0]
            if "last" not in kind:
                window = windowed(updated[-2:], -1 if slab == 0 else 0)
    return assembled(scalars, results)


def solution(mesh):
    sections, lateral, col = mesh.devices.shape
    fine = Mesh(mesh.devices.reshape(sections, lateral, col // 2, 2), ("sec", "lat", "cx", "core"))
    placed = (
        P("sec", ("lat", "cx", "core"), None, None, None),
        P("sec", "lat", ("cx", "core"), None, None, None),
        P("sec", "lat", ("cx", "core")),
        P(),
    )
    return jax.shard_map(
        shards,
        mesh=fine,
        in_specs=placed,
        out_specs=P("sec", ("lat", "cx", "core"), None, None, None),
        check_vma=False,
    )
```

```python
import functools
import math

import jax
import jax.numpy as jnp
from jax import lax
from jax.experimental import pallas as pl
from jax.experimental.pallas import tpu as pltpu
from jax.sharding import Mesh, PartitionSpec as P

OFF = 8
PHASES = 16
REACH = OFF // 2
VMEM_BYTES = 12 * 1024 * 1024

coupling = 0.8

VMEM = pltpu.VMEM
SMEM = pltpu.SMEM
WHOLE = pl.BlockSpec(memory_space=VMEM)
SCALARS = pl.BlockSpec(memory_space=SMEM)


def fold_kernel(rows_all, slab, scalars, pattern, tiles, out):
    row = pl.program_id(0)
    offsets = tiles.shape[2]
    blk = tiles.shape[4]
    index = lax.rem(scalars[0], PHASES)
    cos_value = jnp.float32(1.0)
    sin_value = jnp.float32(0.0)
    for step in range(1, PHASES):
        cos_value = jnp.where(index == step, jnp.float32(math.cos(2 * math.pi * step / PHASES)), cos_value)
        sin_value = jnp.where(index == step, jnp.float32(math.sin(2 * math.pi * step / PHASES)), sin_value)
    for offset in range(offsets):
        origin = scalars[1] + row + scalars[2] + offset - REACH
        below = origin < 0
        above = origin >= rows_all
        mask = pattern[slab, row, offset].astype(jnp.float32)
        real_scale = jnp.where(below | above, cos_value, 1.0) * mask
        imag_scale = jnp.where(below, -sin_value, jnp.where(above, sin_value, 0.0)) * mask
        real_part = tiles[0, 0, offset, 0].astype(jnp.float32)
        imag_part = tiles[0, 0, offset, 1].astype(jnp.float32)
        lanes = pl.ds(offset * blk, blk)
        out[0, pl.ds(0, blk), lanes] = (real_part * real_scale - imag_part * imag_scale).astype(jnp.bfloat16)
        out[0, pl.ds(blk, blk), lanes] = (real_part * imag_scale + imag_part * real_scale).astype(jnp.bfloat16)


def folded_tiles(slab, tiles, pattern, scalars, rows_all):
    _, rows, offsets, _, blk, _ = tiles.shape
    return pl.pallas_call(
        functools.partial(fold_kernel, rows_all, slab),
        grid=(rows,),
        in_specs=[
            SCALARS,
            SCALARS,
            pl.BlockSpec((1, 1, offsets, 2, blk, blk), lambda r: (slab, r, 0, 0, 0, 0)),
        ],
        out_specs=pl.BlockSpec((1, 2 * blk, offsets * blk), lambda r: (r, 0, 0)),
        out_shape=jax.ShapeDtypeStruct((rows, 2 * blk, offsets * blk), jnp.bfloat16),
        compiler_params=pltpu.CompilerParams(vmem_limit_bytes=VMEM_BYTES),
    )(scalars, pattern, tiles)


def step_kernel(kind, reach, pieces, scalars, *refs):
    window, weights, rest = refs[:reach], refs[reach : reach + pieces], refs[reach + pieces : -2]
    taken, held = refs[-2:]
    rows, _, width, blk = window[0].shape
    per_group = weights[0].shape[2] // blk
    skip = -(-REACH // rows) * rows - REACH
    for place in range(OFF + rows - 1):
        taken[place] = window[(place + skip) // rows][(place + skip) % rows].reshape(2 * width, blk)
    starts = [scalars[2 + piece] * per_group for piece in range(pieces)]
    for row in range(rows):
        total = None
        for piece in range(pieces):
            left = jnp.concatenate([taken[starts[piece] + (row + offset)] for offset in range(per_group)], axis=1)
            part = lax.dot_general(
                left, weights[piece][row], (((1,), (1,)), ((), ())), preferred_element_type=jnp.float32
            )
            total = part if total is None else total + part
        product = (total[:width, :blk] - total[width:, blk:], total[:width, blk:] + total[width:, :blk])
        for part in range(2):
            extra = list(rest)
            value = product[part]
            if "add" in kind:
                value = extra.pop(0)[row, part] + coupling * value
            following = value
            if "source" in kind:
                following = extra.pop(0)[row, part].astype(jnp.float32) + coupling * value
            if "merge" in kind:
                value = jnp.where(scalars[0] == kind["merge"], value, extra.pop(0)[row, part])
            if "pieces" in kind:
                held[row, part] = value
                del extra[: kind["pieces"]]
            else:
                extra.pop(0)[row, part] = value
            if "last" not in kind:
                field, edge = extra
                field[row, part] = following.astype(jnp.bfloat16)
                if row < edge.shape[0]:
                    edge[row, part] = following.astype(jnp.bfloat16)
    if "pieces" in kind:
        each = rows // kind["pieces"]
        for by in range(kind["pieces"]):
            goal = lax.rem(scalars[1] + by, kind["pieces"]) * each
            for row in range(each):
                rest[kind["inputs"] + by][row] = held[goal + row]


def applied(kind, scalars, window, weights, extra):
    own = window[0].shape
    rows, height, depth = weights[0].shape
    if "pieces" in kind:
        count = kind["pieces"]
        out_shape = [jax.ShapeDtypeStruct((own[0] // count,) + own[1:], jnp.float32)] * count
    else:
        out_shape = [jax.ShapeDtypeStruct(own, jnp.float32)]
    if "last" not in kind:
        out_shape.append(jax.ShapeDtypeStruct(own, jnp.bfloat16))
        out_shape.append(jax.ShapeDtypeStruct(window[-1].shape, jnp.bfloat16))
    return pl.pallas_call(
        functools.partial(step_kernel, kind | {"inputs": len(extra)}, len(window), len(weights)),
        in_specs=[SCALARS] + [WHOLE] * (len(window) + len(weights) + len(extra)),
        out_specs=[WHOLE] * len(out_shape),
        out_shape=out_shape,
        scratch_shapes=[VMEM((OFF + rows - 1, 2 * own[2], own[3]), jnp.bfloat16), VMEM(own, jnp.float32)],
        compiler_params=pltpu.CompilerParams(vmem_limit_bytes=VMEM_BYTES),
        cost_estimate=pl.CostEstimate(
            flops=2 * own[0] * OFF * 4 * own[2] * own[3] ** 2,
            bytes_accessed=2 * len(weights) * rows * height * depth,
            transcendentals=0,
        ),
    )(scalars, *window, *weights, *extra)


def assembling_kernel(slabs, scalars, *refs):
    pieces, out, held = refs[:-2], refs[-2], refs[-1]
    count = len(pieces) // slabs
    rows = pieces[0].shape[0]
    for slab in range(slabs):
        for by in range(count):
            held[slab, lax.rem(scalars[1] - by + count, count)] = pieces[slab * count + by][...]
    for slab in range(slabs):
        for row in range(rows):
            for part in range(2):
                whole = jnp.concatenate([held[slab, place, row, part] for place in range(count)], axis=0)
                out[slab, row, part] = whole.T


def assembled(scalars, pieces):
    slabs, count = len(pieces), len(pieces[0])
    rows, _, width, blk = pieces[0][0].shape
    return pl.pallas_call(
        functools.partial(assembling_kernel, slabs),
        in_specs=[SCALARS] + [WHOLE] * (slabs * count),
        out_specs=WHOLE,
        out_shape=jax.ShapeDtypeStruct((slabs, rows, 2, blk, width * count), jnp.float32),
        scratch_shapes=[VMEM((slabs, count, rows, 2, width, blk), jnp.float32)],
        compiler_params=pltpu.CompilerParams(vmem_limit_bytes=VMEM_BYTES),
    )(scalars, *[piece for slab in pieces for piece in slab])


def picking_kernel(across, cores, slab, scalars, *refs):
    pieces, out = refs[:-1], refs[-1]
    rows = pieces[0].shape[1]
    for place, piece in enumerate(pieces):
        origin = scalars[2 + place] * rows
        for row in range(rows):
            for part in range(2):
                out[origin + row, part] = piece[slab, row, part, scalars[1]]


def picked(scalars, across, cores, slab, pieces):
    _, rows, _, parts, width, blk = pieces[0].shape
    return pl.pallas_call(
        functools.partial(picking_kernel, across, cores, slab),
        in_specs=[SCALARS] + [WHOLE] * len(pieces),
        out_specs=WHOLE,
        out_shape=jax.ShapeDtypeStruct((rows * parts, 2, width, blk), jnp.bfloat16),
        compiler_params=pltpu.CompilerParams(vmem_limit_bytes=VMEM_BYTES),
    )(scalars, *pieces)


def shifted(value, axis, by):
    size = lax.axis_size(axis)
    return lax.ppermute(value, axis, [((i - by) % size, i) for i in range(size)])


def shards(sources, inverse_tiles, pattern, phase_index):
    sections = lax.axis_size("sec")
    section = lax.axis_index("sec")
    slabs, rows, _, blk, columns = sources.shape
    lateral, across, cores = (lax.axis_size(axis) for axis in ("lat", "cx", "core"))
    cx, core = lax.axis_index("cx"), lax.axis_index("core")
    parts = across * cores
    tile_rows = rows * parts
    width = columns // parts
    scalars = jnp.stack(
        [section, cx * cores + core]
        + [
            lax.rem(cx + (across - by_cx), across) * cores + lax.rem(core + (cores - by_core), cores)
            for by_cx in range(across)
            for by_core in range(cores)
        ]
    ).astype(jnp.int32)
    fold_scalars = jnp.stack(
        [
            phase_index[0],
            lax.axis_index("lat") * tile_rows,
            lax.axis_index(("cx", "core")) * inverse_tiles.shape[2],
        ]
    ).astype(jnp.int32)

    below = -(-REACH // tile_rows)
    above = -(-(OFF - 1 - REACH) // tile_rows)
    edge_rows = OFF - 1 - REACH - (above - 1) * tile_rows

    def windowed(field, by=0):
        window = []
        for shift in range(-below, above + 1):
            pairs = []
            for sec in range(sections):
                origin = (sec - by) % sections * lateral
                pairs += [(origin + (lat + shift) % lateral, sec * lateral + lat) for lat in range(lateral)]
            sent = field[1] if shift == above else field[0]
            window.append(lax.ppermute(sent, ("sec", "lat"), pairs) if by or shift else sent)
        return window

    tiles = []
    folded = [
        folded_tiles(slab, inverse_tiles, pattern, fold_scalars, lateral * tile_rows) for slab in range(slabs)
    ]

    def swapped(near):
        return [shifted(piece, "core", by_core) if by_core else piece for piece in near for by_core in range(cores)]

    def spread(piece):
        return [shifted(piece, "cx", by_cx) if by_cx else piece for by_cx in range(across)]

    around = spread(jnp.swapaxes(sources, 3, 4).reshape(slabs, rows, 2, parts, width, blk))
    around[1:], folded[0] = lax.optimization_barrier((around[1:], folded[0]))
    around = swapped(around)
    turned = [picked(scalars, across, cores, slab, around) for slab in range(slabs)]
    turned[0], folded[1:] = lax.optimization_barrier((turned[0], folded[1:]))
    window = windowed((turned[0], turned[0][:edge_rows]))

    spreads = [spread(piece) for piece in folded]

    def finished(slab, ready):
        near = spreads[slab]
        _, near[1:] = lax.optimization_barrier((ready, near[1:]))
        tiles.append(swapped(near))

    finished(0, window)

    def delivered(pieces):
        received = []
        for by, piece in enumerate(pieces):
            pairs = [(place, (place + by) % parts) for place in range(parts)]
            received.append(lax.ppermute(piece, ("cx", "core"), pairs) if by else piece)
        return received

    values = []
    for turn in range(sections):
        values.append([])
        for slab in range(slabs):
            kind, extra = {}, []
            if turn > 0 and slab == 0:
                kind["add"] = True
                extra.append(values[0][0])
            if slab < slabs - 1:
                kind["source"] = True
                extra.append(turned[slab + 1])
            value, *field = applied(kind, scalars, window, tiles[slab], extra)
            values[turn].append(value)
            last = turn == sections - 1 and slab == slabs - 1
            window = windowed(field, 1 if slab == slabs - 1 and not last else 0)
            if turn == 0 and slab < slabs - 1:
                finished(slab + 1, window)
    results = [None] * slabs
    for turn in range(sections):
        owner = sections - 1 - turn
        for slab in reversed(range(slabs)):
            if turn == 0 and slab == slabs - 1:
                results[slab] = values[owner][slab]
                continue
            kind, extra = {"add": True}, [values[owner][slab]]
            if turn > 0:
                kind["merge"] = owner
                extra.append(results[slab])
            if turn == sections - 1:
                kind["pieces"] = parts
                if slab == 0:
                    kind["last"] = True
            updated = applied(kind, scalars, window, tiles[slab], extra)
            if turn == sections - 1:
                results[slab] = delivered(updated[:parts])
            else:
                results[slab] = updated[0]
            if "last" not in kind:
                window = windowed(updated[-2:], -1 if slab == 0 else 0)
    return assembled(scalars, results)


def solution(mesh):
    sections, lateral, col = mesh.devices.shape
    fine = Mesh(mesh.devices.reshape(sections, lateral, col // 2, 2), ("sec", "lat", "cx", "core"))
    placed = (
        P("sec", ("lat", "cx", "core"), None, None, None),
        P("sec", "lat", ("cx", "core"), None, None, None),
        P("sec", "lat", ("cx", "core")),
        P(),
    )
    return jax.shard_map(
        shards,
        mesh=fine,
        in_specs=placed,
        out_specs=P("sec", ("lat", "cx", "core"), None, None, None),
        check_vma=False,
    )
```

```python
import functools
import math

import jax
import jax.numpy as jnp
from jax import lax
from jax.experimental import pallas as pl
from jax.experimental.pallas import tpu as pltpu
from jax.sharding import Mesh, PartitionSpec as P

OFF = 8
PHASES = 16
REACH = OFF // 2
VMEM_BYTES = 12 * 1024 * 1024

coupling = 0.8

VMEM = pltpu.VMEM
SMEM = pltpu.SMEM
WHOLE = pl.BlockSpec(memory_space=VMEM)
SCALARS = pl.BlockSpec(memory_space=SMEM)


def fold_kernel(rows_all, slab, scalars, pattern, tiles, out, held, arrived):
    rows, offsets, _, blk, _ = held.shape
    copies = [pltpu.make_async_copy(tiles.at[slab, row], held.at[row], arrived.at[row]) for row in range(rows)]
    for copy in copies:
        copy.start()
    index = lax.rem(scalars[0], PHASES)
    cos_value = jnp.float32(1.0)
    sin_value = jnp.float32(0.0)
    for step in range(1, PHASES):
        cos_value = jnp.where(index == step, jnp.float32(math.cos(2 * math.pi * step / PHASES)), cos_value)
        sin_value = jnp.where(index == step, jnp.float32(math.sin(2 * math.pi * step / PHASES)), sin_value)
    for row in range(rows):
        copies[row].wait()
        for offset in range(offsets):
            origin = scalars[1] + row + scalars[2] + offset - REACH
            below = origin < 0
            above = origin >= rows_all
            mask = pattern[slab, row, offset].astype(jnp.float32)
            real_scale = jnp.where(below | above, cos_value, 1.0) * mask
            imag_scale = jnp.where(below, -sin_value, jnp.where(above, sin_value, 0.0)) * mask
            real_part = held[row, offset, 0].astype(jnp.float32)
            imag_part = held[row, offset, 1].astype(jnp.float32)
            lanes = pl.ds(offset * blk, blk)
            out[row, pl.ds(0, blk), lanes] = (real_part * real_scale - imag_part * imag_scale).astype(jnp.bfloat16)
            out[row, pl.ds(blk, blk), lanes] = (real_part * imag_scale + imag_part * real_scale).astype(jnp.bfloat16)


def folded_tiles(slab, tiles, pattern, scalars, rows_all):
    _, rows, offsets, _, blk, _ = tiles.shape
    return pl.pallas_call(
        functools.partial(fold_kernel, rows_all, slab),
        in_specs=[SCALARS, SCALARS, pl.BlockSpec(memory_space=pltpu.HBM)],
        out_specs=WHOLE,
        out_shape=jax.ShapeDtypeStruct((rows, 2 * blk, offsets * blk), jnp.bfloat16),
        scratch_shapes=[VMEM((rows, offsets, 2, blk, blk), jnp.bfloat16), pltpu.SemaphoreType.DMA((rows,))],
        compiler_params=pltpu.CompilerParams(vmem_limit_bytes=VMEM_BYTES),
    )(scalars, pattern, tiles)


def step_kernel(kind, reach, pieces, scalars, *refs):
    window, weights, rest = refs[:reach], refs[reach : reach + pieces], refs[reach + pieces : -2]
    taken, held = refs[-2:]
    rows, _, width, blk = window[0].shape
    per_group = weights[0].shape[2] // blk
    skip = -(-REACH // rows) * rows - REACH
    for place in range(OFF + rows - 1):
        taken[place] = window[(place + skip) // rows][(place + skip) % rows].reshape(2 * width, blk)
    starts = [scalars[2 + piece] * per_group for piece in range(pieces)]
    for row in range(rows):
        total = None
        for piece in range(pieces):
            left = jnp.concatenate([taken[starts[piece] + (row + offset)] for offset in range(per_group)], axis=1)
            part = lax.dot_general(
                left, weights[piece][row], (((1,), (1,)), ((), ())), preferred_element_type=jnp.float32
            )
            total = part if total is None else total + part
        product = (total[:width, :blk] - total[width:, blk:], total[:width, blk:] + total[width:, :blk])
        for part in range(2):
            extra = list(rest)
            value = product[part]
            if "add" in kind:
                value = extra.pop(0)[row, part] + coupling * value
            following = value
            if "source" in kind:
                following = extra.pop(0)[row, part].astype(jnp.float32) + coupling * value
            if "merge" in kind:
                value = jnp.where(scalars[0] == kind["merge"], value, extra.pop(0)[row, part])
            if "pieces" in kind:
                held[row, part] = value
                del extra[: kind["pieces"]]
            else:
                extra.pop(0)[row, part] = value
            if "last" not in kind:
                field, edge = extra
                field[row, part] = following.astype(jnp.bfloat16)
                if row < edge.shape[0]:
                    edge[row, part] = following.astype(jnp.bfloat16)
    if "pieces" in kind:
        each = rows // kind["pieces"]
        for by in range(kind["pieces"]):
            goal = lax.rem(scalars[1] + by, kind["pieces"]) * each
            for row in range(each):
                rest[kind["inputs"] + by][row] = held[goal + row]


def applied(kind, scalars, window, weights, extra):
    own = window[0].shape
    rows, height, depth = weights[0].shape
    if "pieces" in kind:
        count = kind["pieces"]
        out_shape = [jax.ShapeDtypeStruct((own[0] // count,) + own[1:], jnp.float32)] * count
    else:
        out_shape = [jax.ShapeDtypeStruct(own, jnp.float32)]
    if "last" not in kind:
        out_shape.append(jax.ShapeDtypeStruct(own, jnp.bfloat16))
        out_shape.append(jax.ShapeDtypeStruct(window[-1].shape, jnp.bfloat16))
    return pl.pallas_call(
        functools.partial(step_kernel, kind | {"inputs": len(extra)}, len(window), len(weights)),
        in_specs=[SCALARS] + [WHOLE] * (len(window) + len(weights) + len(extra)),
        out_specs=[WHOLE] * len(out_shape),
        out_shape=out_shape,
        scratch_shapes=[VMEM((OFF + rows - 1, 2 * own[2], own[3]), jnp.bfloat16), VMEM(own, jnp.float32)],
        compiler_params=pltpu.CompilerParams(vmem_limit_bytes=VMEM_BYTES),
        cost_estimate=pl.CostEstimate(
            flops=2 * own[0] * OFF * 4 * own[2] * own[3] ** 2,
            bytes_accessed=2 * len(weights) * rows * height * depth,
            transcendentals=0,
        ),
    )(scalars, *window, *weights, *extra)


def assembling_kernel(slabs, scalars, *refs):
    pieces, out, held = refs[:-2], refs[-2], refs[-1]
    count = len(pieces) // slabs
    rows = pieces[0].shape[0]
    for slab in range(slabs):
        for by in range(count):
            held[slab, lax.rem(scalars[1] - by + count, count)] = pieces[slab * count + by][...]
    for slab in range(slabs):
        for row in range(rows):
            for part in range(2):
                whole = jnp.concatenate([held[slab, place, row, part] for place in range(count)], axis=0)
                out[slab, row, part] = whole.T


def assembled(scalars, pieces):
    slabs, count = len(pieces), len(pieces[0])
    rows, _, width, blk = pieces[0][0].shape
    return pl.pallas_call(
        functools.partial(assembling_kernel, slabs),
        in_specs=[SCALARS] + [WHOLE] * (slabs * count),
        out_specs=WHOLE,
        out_shape=jax.ShapeDtypeStruct((slabs, rows, 2, blk, width * count), jnp.float32),
        scratch_shapes=[VMEM((slabs, count, rows, 2, width, blk), jnp.float32)],
        compiler_params=pltpu.CompilerParams(vmem_limit_bytes=VMEM_BYTES),
    )(scalars, *[piece for slab in pieces for piece in slab])


def picking_kernel(across, cores, slab, scalars, *refs):
    pieces, out = refs[:-1], refs[-1]
    rows = pieces[0].shape[1]
    for place, piece in enumerate(pieces):
        origin = scalars[2 + place] * rows
        for row in range(rows):
            for part in range(2):
                out[origin + row, part] = piece[slab, row, part, scalars[1]]


def picked(scalars, across, cores, slab, pieces):
    _, rows, _, parts, width, blk = pieces[0].shape
    return pl.pallas_call(
        functools.partial(picking_kernel, across, cores, slab),
        in_specs=[SCALARS] + [WHOLE] * len(pieces),
        out_specs=WHOLE,
        out_shape=jax.ShapeDtypeStruct((rows * parts, 2, width, blk), jnp.bfloat16),
        compiler_params=pltpu.CompilerParams(vmem_limit_bytes=VMEM_BYTES),
    )(scalars, *pieces)


def shifted(value, axis, by):
    size = lax.axis_size(axis)
    return lax.ppermute(value, axis, [((i - by) % size, i) for i in range(size)])


def shards(sources, inverse_tiles, pattern, phase_index):
    sections = lax.axis_size("sec")
    section = lax.axis_index("sec")
    slabs, rows, _, blk, columns = sources.shape
    lateral, across, cores = (lax.axis_size(axis) for axis in ("lat", "cx", "core"))
    cx, core = lax.axis_index("cx"), lax.axis_index("core")
    parts = across * cores
    tile_rows = rows * parts
    width = columns // parts
    scalars = jnp.stack(
        [section, cx * cores + core]
        + [
            lax.rem(cx + (across - by_cx), across) * cores + lax.rem(core + (cores - by_core), cores)
            for by_cx in range(across)
            for by_core in range(cores)
        ]
    ).astype(jnp.int32)
    fold_scalars = jnp.stack(
        [
            phase_index[0],
            lax.axis_index("lat") * tile_rows,
            lax.axis_index(("cx", "core")) * inverse_tiles.shape[2],
        ]
    ).astype(jnp.int32)

    below = -(-REACH // tile_rows)
    above = -(-(OFF - 1 - REACH) // tile_rows)
    edge_rows = OFF - 1 - REACH - (above - 1) * tile_rows

    def windowed(field, by=0):
        window = []
        for shift in range(-below, above + 1):
            pairs = []
            for sec in range(sections):
                origin = (sec - by) % sections * lateral
                pairs += [(origin + (lat + shift) % lateral, sec * lateral + lat) for lat in range(lateral)]
            sent = field[1] if shift == above else field[0]
            window.append(lax.ppermute(sent, ("sec", "lat"), pairs) if by or shift else sent)
        return window

    tiles = []
    folded = [
        folded_tiles(slab, inverse_tiles, pattern, fold_scalars, lateral * tile_rows) for slab in range(slabs)
    ]

    def swapped(near):
        return [shifted(piece, "core", by_core) if by_core else piece for piece in near for by_core in range(cores)]

    def spread(piece):
        return [shifted(piece, "cx", by_cx) if by_cx else piece for by_cx in range(across)]

    around = spread(jnp.swapaxes(sources, 3, 4).reshape(slabs, rows, 2, parts, width, blk))
    around[1:], folded[0] = lax.optimization_barrier((around[1:], folded[0]))
    around = swapped(around)
    turned = [picked(scalars, across, cores, slab, around) for slab in range(slabs)]
    turned[0], folded[1:] = lax.optimization_barrier((turned[0], folded[1:]))
    window = windowed((turned[0], turned[0][:edge_rows]))

    spreads = [spread(piece) for piece in folded]

    def finished(slab, ready):
        near = spreads[slab]
        _, near[1:] = lax.optimization_barrier((ready, near[1:]))
        tiles.append(swapped(near))

    finished(0, window)

    def delivered(pieces):
        received = []
        for by, piece in enumerate(pieces):
            pairs = [(place, (place + by) % parts) for place in range(parts)]
            received.append(lax.ppermute(piece, ("cx", "core"), pairs) if by else piece)
        return received

    values = []
    for turn in range(sections):
        values.append([])
        for slab in range(slabs):
            kind, extra = {}, []
            if turn > 0 and slab == 0:
                kind["add"] = True
                extra.append(values[0][0])
            if slab < slabs - 1:
                kind["source"] = True
                extra.append(turned[slab + 1])
            value, *field = applied(kind, scalars, window, tiles[slab], extra)
            values[turn].append(value)
            last = turn == sections - 1 and slab == slabs - 1
            window = windowed(field, 1 if slab == slabs - 1 and not last else 0)
            if turn == 0 and slab < slabs - 1:
                finished(slab + 1, window)
    results = [None] * slabs
    for turn in range(sections):
        owner = sections - 1 - turn
        for slab in reversed(range(slabs)):
            if turn == 0 and slab == slabs - 1:
                results[slab] = values[owner][slab]
                continue
            kind, extra = {"add": True}, [values[owner][slab]]
            if turn > 0:
                kind["merge"] = owner
                extra.append(results[slab])
            if turn == sections - 1:
                kind["pieces"] = parts
                if slab == 0:
                    kind["last"] = True
            updated = applied(kind, scalars, window, tiles[slab], extra)
            if turn == sections - 1:
                results[slab] = delivered(updated[:parts])
            else:
                results[slab] = updated[0]
            if "last" not in kind:
                window = windowed(updated[-2:], -1 if slab == 0 else 0)
    return assembled(scalars, results)


def solution(mesh):
    sections, lateral, col = mesh.devices.shape
    fine = Mesh(mesh.devices.reshape(sections, lateral, col // 2, 2), ("sec", "lat", "cx", "core"))
    placed = (
        P("sec", ("lat", "cx", "core"), None, None, None),
        P("sec", "lat", ("cx", "core"), None, None, None),
        P("sec", "lat", ("cx", "core")),
        P(),
    )
    return jax.shard_map(
        shards,
        mesh=fine,
        in_specs=placed,
        out_specs=P("sec", ("lat", "cx", "core"), None, None, None),
        check_vma=False,
    )
```

```python
import functools
import math

import jax
import jax.numpy as jnp
from jax import lax
from jax.experimental import pallas as pl
from jax.experimental.pallas import tpu as pltpu
from jax.sharding import Mesh, PartitionSpec as P

OFF = 8
PHASES = 16
REACH = OFF // 2
VMEM_BYTES = 12 * 1024 * 1024

coupling = 0.8

VMEM = pltpu.VMEM
SMEM = pltpu.SMEM
WHOLE = pl.BlockSpec(memory_space=VMEM)
SCALARS = pl.BlockSpec(memory_space=SMEM)


def fold_kernel(rows_all, slab, scalars, pattern, tiles, out, held, arrived):
    rows, offsets, _, blk, _ = held.shape
    copies = [pltpu.make_async_copy(tiles.at[slab, row], held.at[row], arrived.at[row]) for row in range(rows)]
    for copy in copies:
        copy.start()
    index = lax.rem(scalars[0], PHASES)
    cos_value = jnp.float32(1.0)
    sin_value = jnp.float32(0.0)
    for step in range(1, PHASES):
        cos_value = jnp.where(index == step, jnp.float32(math.cos(2 * math.pi * step / PHASES)), cos_value)
        sin_value = jnp.where(index == step, jnp.float32(math.sin(2 * math.pi * step / PHASES)), sin_value)
    for row in range(rows):
        copies[row].wait()
        for offset in range(offsets):
            origin = scalars[1] + row + scalars[2] + offset - REACH
            below = origin < 0
            above = origin >= rows_all
            mask = pattern[slab, row, offset].astype(jnp.float32)
            real_scale = jnp.where(below | above, cos_value, 1.0) * mask
            imag_scale = jnp.where(below, -sin_value, jnp.where(above, sin_value, 0.0)) * mask
            real_part = held[row, offset, 0].astype(jnp.float32)
            imag_part = held[row, offset, 1].astype(jnp.float32)
            lanes = pl.ds(offset * blk, blk)
            out[row, pl.ds(0, blk), lanes] = (real_part * real_scale - imag_part * imag_scale).astype(jnp.bfloat16)
            out[row, pl.ds(blk, blk), lanes] = (real_part * imag_scale + imag_part * real_scale).astype(jnp.bfloat16)


def folded_tiles(slab, tiles, pattern, scalars, rows_all):
    _, rows, offsets, _, blk, _ = tiles.shape
    return pl.pallas_call(
        functools.partial(fold_kernel, rows_all, slab),
        in_specs=[SCALARS, SCALARS, pl.BlockSpec(memory_space=pl.ANY)],
        out_specs=WHOLE,
        out_shape=jax.ShapeDtypeStruct((rows, 2 * blk, offsets * blk), jnp.bfloat16),
        scratch_shapes=[VMEM((rows, offsets, 2, blk, blk), jnp.bfloat16), pltpu.SemaphoreType.DMA((rows,))],
    )(scalars, pattern, tiles)


def step_kernel(kind, reach, pieces, scalars, *refs):
    window, weights, rest = refs[:reach], refs[reach : reach + pieces], refs[reach + pieces : -2]
    taken, held = refs[-2:]
    rows, _, width, blk = window[0].shape
    per_group = weights[0].shape[2] // blk
    skip = -(-REACH // rows) * rows - REACH
    for place in range(OFF + rows - 1):
        taken[place] = window[(place + skip) // rows][(place + skip) % rows].reshape(2 * width, blk)
    starts = [scalars[2 + piece] * per_group for piece in range(pieces)]
    for row in range(rows):
        total = None
        for piece in range(pieces):
            left = jnp.concatenate([taken[starts[piece] + (row + offset)] for offset in range(per_group)], axis=1)
            part = lax.dot_general(
                left, weights[piece][row], (((1,), (1,)), ((), ())), preferred_element_type=jnp.float32
            )
            total = part if total is None else total + part
        product = (total[:width, :blk] - total[width:, blk:], total[:width, blk:] + total[width:, :blk])
        for part in range(2):
            extra = list(rest)
            value = product[part]
            if "add" in kind:
                value = extra.pop(0)[row, part] + coupling * value
            following = value
            if "source" in kind:
                following = extra.pop(0)[row, part].astype(jnp.float32) + coupling * value
            if "merge" in kind:
                value = jnp.where(scalars[0] == kind["merge"], value, extra.pop(0)[row, part])
            if "pieces" in kind:
                held[row, part] = value
                del extra[: kind["pieces"]]
            else:
                extra.pop(0)[row, part] = value
            if "last" not in kind:
                field, edge = extra
                field[row, part] = following.astype(jnp.bfloat16)
                if row < edge.shape[0]:
                    edge[row, part] = following.astype(jnp.bfloat16)
    if "pieces" in kind:
        each = rows // kind["pieces"]
        for by in range(kind["pieces"]):
            goal = lax.rem(scalars[1] + by, kind["pieces"]) * each
            for row in range(each):
                rest[kind["inputs"] + by][row] = held[goal + row]


def applied(kind, scalars, window, weights, extra):
    own = window[0].shape
    rows, height, depth = weights[0].shape
    if "pieces" in kind:
        count = kind["pieces"]
        out_shape = [jax.ShapeDtypeStruct((own[0] // count,) + own[1:], jnp.float32)] * count
    else:
        out_shape = [jax.ShapeDtypeStruct(own, jnp.float32)]
    if "last" not in kind:
        out_shape.append(jax.ShapeDtypeStruct(own, jnp.bfloat16))
        out_shape.append(jax.ShapeDtypeStruct(window[-1].shape, jnp.bfloat16))
    return pl.pallas_call(
        functools.partial(step_kernel, kind | {"inputs": len(extra)}, len(window), len(weights)),
        in_specs=[SCALARS] + [WHOLE] * (len(window) + len(weights) + len(extra)),
        out_specs=[WHOLE] * len(out_shape),
        out_shape=out_shape,
        scratch_shapes=[VMEM((OFF + rows - 1, 2 * own[2], own[3]), jnp.bfloat16), VMEM(own, jnp.float32)],
        compiler_params=pltpu.CompilerParams(vmem_limit_bytes=VMEM_BYTES),
        cost_estimate=pl.CostEstimate(
            flops=2 * own[0] * OFF * 4 * own[2] * own[3] ** 2,
            bytes_accessed=2 * len(weights) * rows * height * depth,
            transcendentals=0,
        ),
    )(scalars, *window, *weights, *extra)


def assembling_kernel(slabs, scalars, *refs):
    pieces, out, held = refs[:-2], refs[-2], refs[-1]
    count = len(pieces) // slabs
    rows = pieces[0].shape[0]
    for slab in range(slabs):
        for by in range(count):
            held[slab, lax.rem(scalars[1] - by + count, count)] = pieces[slab * count + by][...]
    for slab in range(slabs):
        for row in range(rows):
            for part in range(2):
                whole = jnp.concatenate([held[slab, place, row, part] for place in range(count)], axis=0)
                out[slab, row, part] = whole.T


def assembled(scalars, pieces):
    slabs, count = len(pieces), len(pieces[0])
    rows, _, width, blk = pieces[0][0].shape
    return pl.pallas_call(
        functools.partial(assembling_kernel, slabs),
        in_specs=[SCALARS] + [WHOLE] * (slabs * count),
        out_specs=WHOLE,
        out_shape=jax.ShapeDtypeStruct((slabs, rows, 2, blk, width * count), jnp.float32),
        scratch_shapes=[VMEM((slabs, count, rows, 2, width, blk), jnp.float32)],
        compiler_params=pltpu.CompilerParams(vmem_limit_bytes=VMEM_BYTES),
    )(scalars, *[piece for slab in pieces for piece in slab])


def picking_kernel(across, cores, slab, scalars, *refs):
    pieces, out = refs[:-1], refs[-1]
    rows = pieces[0].shape[1]
    for place, piece in enumerate(pieces):
        origin = scalars[2 + place] * rows
        for row in range(rows):
            for part in range(2):
                out[origin + row, part] = piece[slab, row, part, scalars[1]]


def picked(scalars, across, cores, slab, pieces):
    _, rows, _, parts, width, blk = pieces[0].shape
    return pl.pallas_call(
        functools.partial(picking_kernel, across, cores, slab),
        in_specs=[SCALARS] + [WHOLE] * len(pieces),
        out_specs=WHOLE,
        out_shape=jax.ShapeDtypeStruct((rows * parts, 2, width, blk), jnp.bfloat16),
        compiler_params=pltpu.CompilerParams(vmem_limit_bytes=VMEM_BYTES),
    )(scalars, *pieces)


def shifted(value, axis, by):
    size = lax.axis_size(axis)
    return lax.ppermute(value, axis, [((i - by) % size, i) for i in range(size)])


def shards(sources, inverse_tiles, pattern, phase_index):
    sections = lax.axis_size("sec")
    section = lax.axis_index("sec")
    slabs, rows, _, blk, columns = sources.shape
    lateral, across, cores = (lax.axis_size(axis) for axis in ("lat", "cx", "core"))
    cx, core = lax.axis_index("cx"), lax.axis_index("core")
    parts = across * cores
    tile_rows = rows * parts
    width = columns // parts
    scalars = jnp.stack(
        [section, cx * cores + core]
        + [
            lax.rem(cx + (across - by_cx), across) * cores + lax.rem(core + (cores - by_core), cores)
            for by_cx in range(across)
            for by_core in range(cores)
        ]
    ).astype(jnp.int32)
    fold_scalars = jnp.stack(
        [
            phase_index[0],
            lax.axis_index("lat") * tile_rows,
            lax.axis_index(("cx", "core")) * inverse_tiles.shape[2],
        ]
    ).astype(jnp.int32)

    below = -(-REACH // tile_rows)
    above = -(-(OFF - 1 - REACH) // tile_rows)
    edge_rows = OFF - 1 - REACH - (above - 1) * tile_rows

    def windowed(field, by=0):
        window = []
        for shift in range(-below, above + 1):
            pairs = []
            for sec in range(sections):
                origin = (sec - by) % sections * lateral
                pairs += [(origin + (lat + shift) % lateral, sec * lateral + lat) for lat in range(lateral)]
            sent = field[1] if shift == above else field[0]
            window.append(lax.ppermute(sent, ("sec", "lat"), pairs) if by or shift else sent)
        return window

    tiles = []
    folded = [
        folded_tiles(slab, inverse_tiles, pattern, fold_scalars, lateral * tile_rows) for slab in range(slabs)
    ]

    def swapped(near):
        return [shifted(piece, "core", by_core) if by_core else piece for piece in near for by_core in range(cores)]

    def spread(piece):
        return [shifted(piece, "cx", by_cx) if by_cx else piece for by_cx in range(across)]

    around = spread(jnp.swapaxes(sources, 3, 4).reshape(slabs, rows, 2, parts, width, blk))
    around[1:], folded[0] = lax.optimization_barrier((around[1:], folded[0]))
    around = swapped(around)
    turned = [picked(scalars, across, cores, slab, around) for slab in range(slabs)]
    turned[0], folded[1:] = lax.optimization_barrier((turned[0], folded[1:]))
    window = windowed((turned[0], turned[0][:edge_rows]))

    spreads = [spread(piece) for piece in folded]

    def finished(slab, ready):
        near = spreads[slab]
        _, near[1:] = lax.optimization_barrier((ready, near[1:]))
        tiles.append(swapped(near))

    finished(0, window)

    def delivered(pieces):
        received = []
        for by, piece in enumerate(pieces):
            pairs = [(place, (place + by) % parts) for place in range(parts)]
            received.append(lax.ppermute(piece, ("cx", "core"), pairs) if by else piece)
        return received

    values = []
    for turn in range(sections):
        values.append([])
        for slab in range(slabs):
            kind, extra = {}, []
            if turn > 0 and slab == 0:
                kind["add"] = True
                extra.append(values[0][0])
            if slab < slabs - 1:
                kind["source"] = True
                extra.append(turned[slab + 1])
            value, *field = applied(kind, scalars, window, tiles[slab], extra)
            values[turn].append(value)
            last = turn == sections - 1 and slab == slabs - 1
            window = windowed(field, 1 if slab == slabs - 1 and not last else 0)
            if turn == 0 and slab < slabs - 1:
                finished(slab + 1, window)
    results = [None] * slabs
    for turn in range(sections):
        owner = sections - 1 - turn
        for slab in reversed(range(slabs)):
            if turn == 0 and slab == slabs - 1:
                results[slab] = values[owner][slab]
                continue
            kind, extra = {"add": True}, [values[owner][slab]]
            if turn > 0:
                kind["merge"] = owner
                extra.append(results[slab])
            if turn == sections - 1:
                kind["pieces"] = parts
                if slab == 0:
                    kind["last"] = True
            updated = applied(kind, scalars, window, tiles[slab], extra)
            if turn == sections - 1:
                results[slab] = delivered(updated[:parts])
            else:
                results[slab] = updated[0]
            if "last" not in kind:
                window = windowed(updated[-2:], -1 if slab == 0 else 0)
    return assembled(scalars, results)


def solution(mesh):
    sections, lateral, col = mesh.devices.shape
    fine = Mesh(mesh.devices.reshape(sections, lateral, col // 2, 2), ("sec", "lat", "cx", "core"))
    placed = (
        P("sec", ("lat", "cx", "core"), None, None, None),
        P("sec", "lat", ("cx", "core"), None, None, None),
        P("sec", "lat", ("cx", "core")),
        P(),
    )
    return jax.shard_map(
        shards,
        mesh=fine,
        in_specs=placed,
        out_specs=P("sec", ("lat", "cx", "core"), None, None, None),
        check_vma=False,
    )
```

```python
import functools
import math

import jax
import jax.numpy as jnp
from jax import lax
from jax.experimental import pallas as pl
from jax.experimental.pallas import tpu as pltpu
from jax.sharding import Mesh, PartitionSpec as P

OFF = 8
PHASES = 16
REACH = OFF // 2
VMEM_BYTES = 12 * 1024 * 1024

coupling = 0.8

VMEM = pltpu.VMEM
SMEM = pltpu.SMEM
WHOLE = pl.BlockSpec(memory_space=VMEM)
SCALARS = pl.BlockSpec(memory_space=SMEM)


def fold_kernel(rows_all, slab, scalars, pattern, tiles, out):
    row = pl.program_id(0)
    offsets = tiles.shape[2]
    blk = tiles.shape[4]
    index = lax.rem(scalars[0], PHASES)
    cos_value = jnp.float32(1.0)
    sin_value = jnp.float32(0.0)
    for step in range(1, PHASES):
        cos_value = jnp.where(index == step, jnp.float32(math.cos(2 * math.pi * step / PHASES)), cos_value)
        sin_value = jnp.where(index == step, jnp.float32(math.sin(2 * math.pi * step / PHASES)), sin_value)
    for offset in range(offsets):
        origin = scalars[1] + row + scalars[2] + offset - REACH
        below = origin < 0
        above = origin >= rows_all
        mask = pattern[slab, row, offset].astype(jnp.float32)
        real_scale = jnp.where(below | above, cos_value, 1.0) * mask
        imag_scale = jnp.where(below, -sin_value, jnp.where(above, sin_value, 0.0)) * mask
        real_part = tiles[0, 0, offset, 0].astype(jnp.float32)
        imag_part = tiles[0, 0, offset, 1].astype(jnp.float32)
        lanes = pl.ds(offset * blk, blk)
        out[0, pl.ds(0, blk), lanes] = (real_part * real_scale - imag_part * imag_scale).astype(jnp.bfloat16)
        out[0, pl.ds(blk, blk), lanes] = (real_part * imag_scale + imag_part * real_scale).astype(jnp.bfloat16)


def folded_tiles(slab, tiles, pattern, scalars, rows_all):
    _, rows, offsets, _, blk, _ = tiles.shape
    return pl.pallas_call(
        functools.partial(fold_kernel, rows_all, slab),
        grid=(rows,),
        in_specs=[
            SCALARS,
            SCALARS,
            pl.BlockSpec((1, 1, offsets, 2, blk, blk), lambda r: (slab, r, 0, 0, 0, 0)),
        ],
        out_specs=pl.BlockSpec((1, 2 * blk, offsets * blk), lambda r: (r, 0, 0)),
        out_shape=jax.ShapeDtypeStruct((rows, 2 * blk, offsets * blk), jnp.bfloat16),
        compiler_params=pltpu.CompilerParams(vmem_limit_bytes=VMEM_BYTES),
    )(scalars, pattern, tiles)


def step_kernel(kind, reach, pieces, scalars, *refs):
    window, weights, rest = refs[:reach], refs[reach : reach + pieces], refs[reach + pieces : -2]
    taken, held = refs[-2:]
    rows, _, width, blk = window[0].shape
    per_group = weights[0].shape[2] // blk
    skip = -(-REACH // rows) * rows - REACH
    for place in range(OFF + rows - 1):
        taken[place] = window[(place + skip) // rows][(place + skip) % rows].reshape(2 * width, blk)
    starts = [scalars[2 + piece] * per_group for piece in range(pieces)]
    for row in range(rows):
        total = None
        for piece in range(pieces):
            left = jnp.concatenate([taken[starts[piece] + (row + offset)] for offset in range(per_group)], axis=1)
            part = lax.dot_general(
                left, weights[piece][row], (((1,), (1,)), ((), ())), preferred_element_type=jnp.float32
            )
            total = part if total is None else total + part
        product = (total[:width, :blk] - total[width:, blk:], total[:width, blk:] + total[width:, :blk])
        for part in range(2):
            extra = list(rest)
            value = product[part]
            if "add" in kind:
                value = extra.pop(0)[row, part] + coupling * value
            following = value
            if "source" in kind:
                following = extra.pop(0)[row, part].astype(jnp.float32) + coupling * value
            if "merge" in kind:
                value = jnp.where(scalars[0] == kind["merge"], value, extra.pop(0)[row, part])
            if "pieces" in kind:
                held[row, part] = value
            else:
                extra.pop(0)[row, part] = value
            if "last" not in kind:
                field, edge = extra
                field[row, part] = following.astype(jnp.bfloat16)
                if row < edge.shape[0]:
                    edge[row, part] = following.astype(jnp.bfloat16)
    if "pieces" in kind:
        each = rows // kind["pieces"]
        results = (held,) + tuple(rest[kind["inputs"] - kind["others"] : kind["inputs"]])
        for by in range(kind["pieces"]):
            goal = lax.rem(scalars[1] + by, kind["pieces"]) * each
            for slab, result in enumerate(results):
                for row in range(each):
                    rest[kind["inputs"] + by][slab, row] = result[goal + row].astype(jnp.bfloat16)


def applied(kind, scalars, window, weights, extra):
    own = window[0].shape
    rows, height, depth = weights[0].shape
    if "pieces" in kind:
        count = kind["pieces"]
        out_shape = [
            jax.ShapeDtypeStruct((1 + kind["others"], own[0] // count) + own[1:], jnp.bfloat16)
        ] * count
    else:
        out_shape = [jax.ShapeDtypeStruct(own, jnp.float32)]
    if "last" not in kind:
        out_shape.append(jax.ShapeDtypeStruct(own, jnp.bfloat16))
        out_shape.append(jax.ShapeDtypeStruct(window[-1].shape, jnp.bfloat16))
    return pl.pallas_call(
        functools.partial(step_kernel, kind | {"inputs": len(extra)}, len(window), len(weights)),
        in_specs=[SCALARS] + [WHOLE] * (len(window) + len(weights) + len(extra)),
        out_specs=[WHOLE] * len(out_shape),
        out_shape=out_shape,
        scratch_shapes=[VMEM((OFF + rows - 1, 2 * own[2], own[3]), jnp.bfloat16), VMEM(own, jnp.float32)],
        compiler_params=pltpu.CompilerParams(vmem_limit_bytes=VMEM_BYTES),
        cost_estimate=pl.CostEstimate(
            flops=2 * own[0] * OFF * 4 * own[2] * own[3] ** 2,
            bytes_accessed=2 * len(weights) * rows * height * depth,
            transcendentals=0,
        ),
    )(scalars, *window, *weights, *extra)


def assembling_kernel(scalars, *refs):
    pieces, out, held = refs[:-2], refs[-2], refs[-1]
    count = len(pieces)
    for by in range(count):
        held[lax.rem(scalars[1] - by + count, count)] = pieces[by][...].astype(jnp.float32)
    for slab in range(out.shape[0]):
        for row in range(out.shape[1]):
            for part in range(2):
                whole = jnp.concatenate([held[place, slab, row, part] for place in range(count)], axis=0)
                out[slab, row, part] = whole.T


def assembled(scalars, pieces):
    slabs, rows, _, width, blk = pieces[0].shape
    count = len(pieces)
    return pl.pallas_call(
        assembling_kernel,
        in_specs=[SCALARS] + [WHOLE] * count,
        out_specs=WHOLE,
        out_shape=jax.ShapeDtypeStruct((slabs, rows, 2, blk, width * count), jnp.float32),
        scratch_shapes=[VMEM((count, slabs, rows, 2, width, blk), jnp.float32)],
        compiler_params=pltpu.CompilerParams(vmem_limit_bytes=VMEM_BYTES),
    )(scalars, *pieces)


def picking_kernel(across, cores, slab, scalars, *refs):
    pieces, out = refs[:-1], refs[-1]
    rows = pieces[0].shape[1]
    for place, piece in enumerate(pieces):
        origin = scalars[2 + place] * rows
        for row in range(rows):
            for part in range(2):
                out[origin + row, part] = piece[slab, row, part, scalars[1]]


def picked(scalars, across, cores, slab, pieces):
    _, rows, _, parts, width, blk = pieces[0].shape
    return pl.pallas_call(
        functools.partial(picking_kernel, across, cores, slab),
        in_specs=[SCALARS] + [WHOLE] * len(pieces),
        out_specs=WHOLE,
        out_shape=jax.ShapeDtypeStruct((rows * parts, 2, width, blk), jnp.bfloat16),
        compiler_params=pltpu.CompilerParams(vmem_limit_bytes=VMEM_BYTES),
    )(scalars, *pieces)


def shifted(value, axis, by):
    size = lax.axis_size(axis)
    return lax.ppermute(value, axis, [((i - by) % size, i) for i in range(size)])


def shards(sources, inverse_tiles, pattern, phase_index):
    sections = lax.axis_size("sec")
    section = lax.axis_index("sec")
    slabs, rows, _, blk, columns = sources.shape
    lateral, across, cores = (lax.axis_size(axis) for axis in ("lat", "cx", "core"))
    cx, core = lax.axis_index("cx"), lax.axis_index("core")
    parts = across * cores
    tile_rows = rows * parts
    width = columns // parts
    scalars = jnp.stack(
        [section, cx * cores + core]
        + [
            lax.rem(cx + (across - by_cx), across) * cores + lax.rem(core + (cores - by_core), cores)
            for by_cx in range(across)
            for by_core in range(cores)
        ]
    ).astype(jnp.int32)
    fold_scalars = jnp.stack(
        [
            phase_index[0],
            lax.axis_index("lat") * tile_rows,
            lax.axis_index(("cx", "core")) * inverse_tiles.shape[2],
        ]
    ).astype(jnp.int32)

    below = -(-REACH // tile_rows)
    above = -(-(OFF - 1 - REACH) // tile_rows)
    edge_rows = OFF - 1 - REACH - (above - 1) * tile_rows

    def windowed(field, by=0):
        window = []
        for shift in range(-below, above + 1):
            pairs = []
            for sec in range(sections):
                origin = (sec - by) % sections * lateral
                pairs += [(origin + (lat + shift) % lateral, sec * lateral + lat) for lat in range(lateral)]
            sent = field[1] if shift == above else field[0]
            window.append(lax.ppermute(sent, ("sec", "lat"), pairs) if by or shift else sent)
        return window

    tiles = []
    folded = [
        folded_tiles(slab, inverse_tiles, pattern, fold_scalars, lateral * tile_rows) for slab in range(slabs)
    ]

    def swapped(near):
        return [shifted(piece, "core", by_core) if by_core else piece for piece in near for by_core in range(cores)]

    def spread(piece):
        return [shifted(piece, "cx", by_cx) if by_cx else piece for by_cx in range(across)]

    around = spread(jnp.swapaxes(sources, 3, 4).reshape(slabs, rows, 2, parts, width, blk))
    around[1:], folded[0] = lax.optimization_barrier((around[1:], folded[0]))
    around = swapped(around)
    turned = [picked(scalars, across, cores, slab, around) for slab in range(slabs)]
    turned[0], folded[1:] = lax.optimization_barrier((turned[0], folded[1:]))
    window = windowed((turned[0], turned[0][:edge_rows]))

    spreads = [spread(piece) for piece in folded]

    def finished(slab, ready):
        near = spreads[slab]
        _, near[1:] = lax.optimization_barrier((ready, near[1:]))
        tiles.append(swapped(near))

    finished(0, window)

    def delivered(pieces):
        received = []
        for by, piece in enumerate(pieces):
            pairs = [(place, (place + by) % parts) for place in range(parts)]
            received.append(lax.ppermute(piece, ("cx", "core"), pairs) if by else piece)
        return received

    values = []
    for turn in range(sections):
        values.append([])
        for slab in range(slabs):
            kind, extra = {}, []
            if turn > 0 and slab == 0:
                kind["add"] = True
                extra.append(values[0][0])
            if slab < slabs - 1:
                kind["source"] = True
                extra.append(turned[slab + 1])
            value, *field = applied(kind, scalars, window, tiles[slab], extra)
            values[turn].append(value)
            last = turn == sections - 1 and slab == slabs - 1
            window = windowed(field, 1 if slab == slabs - 1 and not last else 0)
            if turn == 0 and slab < slabs - 1:
                finished(slab + 1, window)
    results = [None] * slabs
    for turn in range(sections):
        owner = sections - 1 - turn
        for slab in reversed(range(slabs)):
            if turn == 0 and slab == slabs - 1:
                results[slab] = values[owner][slab]
                continue
            kind, extra = {"add": True}, [values[owner][slab]]
            if turn > 0:
                kind["merge"] = owner
                extra.append(results[slab])
            if turn == sections - 1 and slab == 0:
                kind["last"] = True
                kind["pieces"] = parts
                kind["others"] = slabs - 1
                extra += results[1:]
            updated = applied(kind, scalars, window, tiles[slab], extra)
            results[slab] = updated[0]
            if "last" not in kind:
                window = windowed(updated[-2:], -1 if slab == 0 else 0)
    return assembled(scalars, delivered(updated))


def solution(mesh):
    sections, lateral, col = mesh.devices.shape
    fine = Mesh(mesh.devices.reshape(sections, lateral, col // 2, 2), ("sec", "lat", "cx", "core"))
    placed = (
        P("sec", ("lat", "cx", "core"), None, None, None),
        P("sec", "lat", ("cx", "core"), None, None, None),
        P("sec", "lat", ("cx", "core")),
        P(),
    )
    return jax.shard_map(
        shards,
        mesh=fine,
        in_specs=placed,
        out_specs=P("sec", ("lat", "cx", "core"), None, None, None),
        check_vma=False,
    )
```
